128 devices in a mesh: chan: 4 (over z_lo, core), blk: 32 (over x, z_hi, y).
Axes of the slice: x: 4, y: 4, z: 4 (z_hi: 2, z_lo: 2; z = z_hi * 2 + z_lo), core: 2. Of those that a mesh axis runs over, the one named last changes fastest.
Arguments:
- voltages: bfloat16 [4096, 2, 2, 4336], P(('blk', 'chan')), may hold values from -6 to 6
- filter_taps: float32 [16, 16], replicated, may hold values from -1.5 to 1.5
- sample_counts: int32 [4096, 2], P(('blk', 'chan')), may hold values from 1084 to 4336
- keep_list: int32 [128, 4, 24], P(('blk', 'chan')), may hold values from 0 to 32, as said below
Outputs:
- visibility: float32 [2, 32, 4096, 2176], P(None, 'chan', 'blk')
The draws below stay inside these ranges and needn't reach their ends.
Inputs may be any that keep to these rules, and one draw needn't show every extreme that they name: keep_list[s, g, :] holds, in increasing order, distinct indices within source block s (below 32) of the inputs unflagged for channel group g, then 32 in every unused slot; each list has 12 to 24 indices, and in every draw, for some channel group, the 4 source blocks s with the same s // 4 all list 24 indices.
All inputs are finite; a program needn't handle non-finite values.
Results may differ from the reference program's by a relative error of at most 0.0035.
Values may be sent and summed in bfloat16 or wider, within the bound.
No kernel may reach another device: no remote copies, remote signals or barrier semaphores. Data moves between devices by JAX's collectives and lax.ppermute only.
A program may use at most 320 MiB of HBM per device.

```python
import math
import jax
import jax.numpy as jnp
from jax import lax

RECEIVER_FEEDS = 4096
COARSE = 2
FFT = 16
TAPS = 16
SPECTRA = 256
CAP = 24
FINE = 32
SUBBANDS_EACH = 8
SRC_BLOCKS = 128
IN_SRC = 32
BLKIN = 128
HALF = 17
TIME_STEPS = 4336
N_CHAN = 4
N_BLK = 32


def draw_keep_list(key, part):
    key_count, key_block, key_group, key_order = jax.random.split(key, 4)
    counts = jax.random.randint(key_count, (SRC_BLOCKS, N_CHAN), CAP // 2, CAP + 1)
    full_block = jax.random.randint(key_block, (), 0, N_BLK)
    full_group = jax.random.randint(key_group, (), 0, N_CHAN)
    source_ids = jnp.arange(SRC_BLOCKS)
    forced = (source_ids // N_CHAN == full_block)[:, None] & (jnp.arange(N_CHAN) == full_group)[None, :]
    counts = jnp.where(forced, CAP, counts)
    positions = jnp.arange(IN_SRC)
    scores = jax.random.randint(key_order, (SRC_BLOCKS, N_CHAN, IN_SRC), 0, 1 << 20) * IN_SRC + positions
    rank_of = jnp.argsort(jnp.argsort(scores, axis=-1), axis=-1)
    chosen = rank_of < counts[:, :, None]
    order_keys = jnp.where(chosen, 0, IN_SRC) + positions
    listed = jnp.argsort(order_keys, axis=-1)[:, :, :CAP]
    slot_index = jnp.arange(CAP)
    return jnp.where(slot_index < counts[:, :, None], listed, IN_SRC).astype(jnp.int32)


def plant(values, stream_key, smallest, high):
    longest = values.shape.index(max(values.shape))
    spots = []
    for shift in (0, 1):
        where = [jax.random.randint(jax.random.fold_in(stream_key, axis), (), 0, length) for axis, length in enumerate(values.shape)]
        where[longest] = (where[longest] + shift) % values.shape[longest]
        spots.append(tuple(where))
    return values.at[spots[0]].set(smallest).at[spots[1]].set(high)


def block_scale(stream_key, shape, pieces, low, high):
    def one(position, blocks):
        draws = jax.random.uniform(jax.random.fold_in(jax.random.fold_in(stream_key, 6), position), (blocks,), jnp.float32, low / len(pieces), high / len(pieces))
        return jnp.repeat(jnp.exp(draws), shape[position] // blocks).reshape((-1,) + (1,) * (len(shape) - position - 1))

    level = one(*pieces[0])
    for cut in pieces[1:]:
        level = level * one(*cut)
    return level


def bell_draw(stream_key, extent, deviation, limit, cuts=(), kind=jnp.bfloat16):
    loudness = block_scale(stream_key, extent, cuts, -0.22, 0.18) if cuts else 1.0
    array = jax.random.normal(stream_key, extent, jnp.float32) * deviation * loudness
    return jnp.minimum(jnp.maximum(array, -limit), limit).astype(kind)


def setup_inputs(seed: int = 0) -> dict:
    key_of = jax.random.split(jax.random.key(seed), 5)
    voltages = bell_draw(key_of[0], (RECEIVER_FEEDS, COARSE, 2, TIME_STEPS), 1.0, 6.0, ((0, 128),))
    filter_taps = bell_draw(key_of[1], (TAPS, FFT), TAPS ** -0.5, 1.5, (), jnp.float32)
    sample_counts = plant(jax.random.randint(key_of[2], (RECEIVER_FEEDS, COARSE), TIME_STEPS // 4, TIME_STEPS + 1), jax.random.fold_in(key_of[2], 1), TIME_STEPS // 4, TIME_STEPS).astype(jnp.int32)
    keep_list = draw_keep_list(jax.random.fold_in(key_of[4], 71), 0)
    return dict(voltages=voltages, filter_taps=filter_taps, sample_counts=sample_counts, keep_list=keep_list)


def filter_bank(voltages, filter_taps, sample_counts, spectra_len):
    in_count, coarse, _, samples = voltages.shape
    tap_count, fft_len = filter_taps.shape
    frames = voltages.astype(jnp.float32).reshape(in_count, coarse, 2, samples // fft_len, fft_len)
    filtered = frames[:, :, :, 0:spectra_len, :] * filter_taps[0]
    for tap_index in range(1, tap_count):
        filtered = filtered + frames[:, :, :, tap_index:tap_index + spectra_len, :] * filter_taps[tap_index]
    bin_index = jnp.arange(fft_len, dtype=jnp.int32)
    phase_angle = 2.0 * math.pi / fft_len * (bin_index[:, None] * bin_index[None, :] % fft_len).astype(jnp.float32)
    cosine = jnp.cos(phase_angle)
    sine_table = jnp.sin(phase_angle)
    cosine_component_source = filtered[:, :, 0]
    imaginary_input = filtered[:, :, 1]
    highest = lax.Precision.HIGHEST
    real_out = jnp.einsum('ictp,fp->icft', cosine_component_source, cosine, precision=highest) + jnp.einsum('ictp,fp->icft', imaginary_input, sine_table, precision=highest)
    imag_out = jnp.einsum('ictp,fp->icft', imaginary_input, cosine, precision=highest) - jnp.einsum('ictp,fp->icft', cosine_component_source, sine_table, precision=highest)
    rescale = jnp.sqrt(samples / (fft_len * sample_counts.astype(jnp.float32)))
    spectra = jnp.stack([real_out, imag_out], axis=3) * rescale[:, :, None, None, None]
    return spectra.reshape(in_count, coarse * fft_len, 2, spectra_len).astype(jnp.bfloat16)

def reference(voltages, filter_taps, sample_counts, keep_list):
    spectra_all = filter_bank(voltages, filter_taps, sample_counts, SPECTRA)
    positions = jnp.arange(IN_SRC, dtype=jnp.int32)
    cluster_assignment = lax.optimization_barrier(jnp.sum((keep_list[:, :, :, None] == positions).astype(jnp.float32), axis=2))
    spectral_keep_mask = jnp.transpose(cluster_assignment, (1, 0, 2)).reshape(N_CHAN, RECEIVER_FEEDS)
    row_block = jnp.arange(N_BLK, dtype=jnp.int32)[:, None]
    col_index = jnp.arange(HALF * BLKIN, dtype=jnp.int32)[None, :]
    column_index = (row_block + col_index // BLKIN) % N_BLK * BLKIN + col_index % BLKIN
    column_index = jnp.broadcast_to(column_index[:, None, :], (N_BLK, BLKIN, HALF * BLKIN))
    highest = lax.Precision.HIGHEST
    normalize = 1.0 / math.sqrt(SPECTRA)

    def pick_columns(full_matrix):
        picked = jnp.take_along_axis(full_matrix.reshape(N_BLK, BLKIN, RECEIVER_FEEDS), column_index, axis=2)
        return picked.reshape(RECEIVER_FEEDS, HALF * BLKIN) * normalize

    def one_channel(subband_position):
        channel_data = lax.dynamic_index_in_dim(spectra_all, subband_position, 1, keepdims=False).astype(jnp.float32)
        window_coefficient_vector = lax.dynamic_index_in_dim(spectral_keep_mask, subband_position // SUBBANDS_EACH, 0, keepdims=False)
        channel_data = channel_data * window_coefficient_vector[:, None, None]
        real_part = channel_data[:, 0]
        imag_part = channel_data[:, 1]
        real_vis = jnp.dot(real_part, real_part.T, precision=highest) + jnp.dot(imag_part, imag_part.T, precision=highest)
        imag_vis = jnp.dot(imag_part, real_part.T, precision=highest) - jnp.dot(real_part, imag_part.T, precision=highest)
        return (pick_columns(real_vis), pick_columns(imag_vis))
    real_all, imag_all = lax.map(one_channel, jnp.arange(FINE, dtype=jnp.int32))
    return jnp.stack([real_all, imag_all])
```

```python
import math

import jax
import jax.numpy as jnp
import numpy as np
from jax import lax
from jax.experimental import pallas as pl
from jax.experimental.pallas import tpu as pltpu
from jax.sharding import Mesh
from jax.sharding import PartitionSpec as P

TAPS = 16
FFT = 16
STEP = 8
LANES = 128
CHUNKS = LANES // STEP


def trig_table():
    table = np.zeros((2, 2, LANES, 8, 2, STEP), np.float64)
    point = np.arange(LANES) % FFT
    for half in range(2):
        for fine in range(8):
            angle = 2.0 * math.pi * ((8 * half + fine) * point % FFT) / FFT
            cosine, sine = np.cos(angle)[:, None], np.sin(angle)[:, None]
            table[half, 0, :, fine, 0] = cosine
            table[half, 0, :, fine, 1] = -sine
            table[half, 1, :, fine, 0] = sine
            table[half, 1, :, fine, 1] = cosine
    return table.reshape(2, 2 * LANES, LANES).astype(np.float32)


def channelize_kernel(spectra_len, cap, volt, rows, scale, taps, trig, out, frames, weights):
    samples = volt.shape[1]
    tiles = -(-samples // LANES)
    listed = 2 * cap
    point_row = lax.broadcasted_iota(jnp.int32, (LANES, LANES), 0) // FFT
    spec_lane = lax.broadcasted_iota(jnp.int32, (LANES, LANES), 1) % STEP
    lag = point_row - spec_lane
    column = [jnp.broadcast_to(taps[:, m : m + 1], (LANES, LANES)) for m in range(TAPS)]
    for part in range(3):
        shaped = jnp.zeros((LANES, LANES), jnp.float32)
        for m in range(TAPS):
            shaped = jnp.where(lag == m - STEP * part, column[m], shaped)
        both = jnp.concatenate([shaped, shaped], axis=0)
        for half in range(2):
            exact = both * trig[half]
            high = exact.astype(jnp.bfloat16)
            low = (exact - high.astype(jnp.float32)).astype(jnp.bfloat16)
            weights[half, part, :, 0:LANES] = high
            weights[half, part, :, LANES : 2 * LANES] = low
    wanted = rows[...] == lax.broadcasted_iota(jnp.int32, (4 * listed, LANES), 1)
    pick = wanted.astype(jnp.bfloat16)
    for tile in range(tiles):
        width = min(LANES, samples - tile * LANES)
        piece = volt[:, tile * LANES : tile * LANES + width]
        if width < LANES:
            piece = jnp.concatenate([piece, jnp.zeros((LANES, LANES - width), piece.dtype)], axis=1)
        got = jnp.dot(pick, piece, preferred_element_type=jnp.float32).astype(jnp.bfloat16)
        for half in range(2):
            base = 2 * half * listed
            here = slice(tile * listed, (tile + 1) * listed)
            frames[half, here, 0:LANES] = got[base : base + listed]
            frames[half, here, LANES : 2 * LANES] = got[base + listed : base + 2 * listed]
    factor = jnp.sum(jnp.where(wanted, scale[...], 0.0), axis=1, keepdims=True)
    chunk = lax.broadcasted_iota(jnp.int32, (listed, LANES), 1) // STEP
    for half in range(2):
        gain = factor[2 * half * listed : (2 * half + 1) * listed]
        for quarter in range(spectra_len // LANES):
            total = None
            for part in range(3):
                first = (quarter * CHUNKS + part) * listed
                term = jnp.dot(
                    frames[half, first : first + CHUNKS * listed, :],
                    weights[half, part],
                    preferred_element_type=jnp.float32,
                )
                total = term if total is None else total + term
            summed = total[:, 0:LANES] + total[:, LANES : 2 * LANES]
            lines = [summed[n * listed : (n + 1) * listed] * gain for n in range(CHUNKS)]
            bit = 1
            while bit < CHUNKS:
                keep = (chunk & bit) == 0
                fresh = list(lines)
                for n in range(CHUNKS):
                    if n & bit == 0:
                        one, two = lines[n], lines[n | bit]
                        fresh[n] = jnp.where(keep, one, pltpu.roll(two, bit * STEP, 1))
                        fresh[n | bit] = jnp.where(keep, pltpu.roll(one, LANES - bit * STEP, 1), two)
                lines = fresh
                bit *= 2
            for n in range(CHUNKS):
                fine, part = divmod(n, 2)
                lane = (fine * 2 + part) * spectra_len + quarter * LANES
                value = lines[n].astype(jnp.bfloat16)
                out[half, :, lane : lane + LANES] = value[0:cap]
                out[half + 2, :, lane : lane + LANES] = value[cap : 2 * cap]


def channelize(voltages, filter_taps, sample_counts, flag_lists, spectra_len):
    in_count, coarse, _, samples = voltages.shape
    groups, cap = flag_lists.shape
    volt = voltages.reshape(in_count * coarse * 2, samples)
    by_half = jnp.transpose(flag_lists.reshape(2, 2, cap), (1, 0, 2))
    rows = (
        by_half[:, None] * (2 * coarse)
        + 2 * jnp.arange(2, dtype=jnp.int32)[None, None, :, None]
        + jnp.arange(2, dtype=jnp.int32)[None, :, None, None]
    ).reshape(8 * cap, 1)
    gain = jnp.sqrt(samples / (FFT * sample_counts.astype(jnp.float32)))
    gain = jnp.repeat(gain.reshape(-1), 2).reshape(1, -1)
    taps = jnp.tile(filter_taps.T, (LANES // FFT, 1))
    row_width = 8 * 2 * spectra_len
    tiles = -(-samples // LANES)

    def kernel(*refs):
        channelize_kernel(spectra_len, cap, *refs)

    return pl.pallas_call(
        kernel,
        out_shape=jax.ShapeDtypeStruct((groups, cap, row_width), jnp.bfloat16),
        scratch_shapes=[
            pltpu.VMEM((2, tiles * 2 * cap, 2 * LANES), jnp.bfloat16),
            pltpu.VMEM((2, 3, 2 * LANES, 2 * LANES), jnp.bfloat16),
        ],
        compiler_params=pltpu.CompilerParams(vmem_limit_bytes=48 * 1024 * 1024),
        cost_estimate=pl.CostEstimate(flops=4 * 10**9, bytes_accessed=3 * 10**6, transcendentals=0),
        name="channelize",
    )(volt, rows, gain, taps, trig_table())


def place_rows(block, where):
    inputs = LANES
    spots = lax.broadcasted_iota(jnp.int32, (inputs, block.shape[0]), 0)
    one_hot = (spots == where).astype(jnp.bfloat16)
    return jnp.dot(one_hot, block, preferred_element_type=jnp.float32).astype(jnp.bfloat16)


def own_kernel(fine, norm, where_all, block, sides, out):
    width = block.shape[1] // fine
    half = width // 2
    for f in range(fine):
        full = place_rows(block[:, f * width : (f + 1) * width], where_all[0])
        scaled = (full.astype(jnp.float32) * norm).astype(jnp.bfloat16)
        turned = jnp.concatenate([scaled[:, half:], -scaled[:, :half]], axis=1)
        both = jnp.concatenate([scaled, turned], axis=0)
        sides[:, f * width : (f + 1) * width] = both
        got = lax.dot_general(both, full, (((1,), (1,)), ((), ())), preferred_element_type=jnp.float32)
        out[0, f] = got[0:LANES]
        out[1, f] = got[LANES : 2 * LANES]


def pair_kernel(fine, spots, where_all, sides, block, _, out):
    width = block.shape[1] // fine
    for f in range(fine):
        full = place_rows(block[:, f * width : (f + 1) * width], where_all[0])
        got = lax.dot_general(
            sides[:, f * width : (f + 1) * width],
            full,
            (((1,), (1,)), ((), ())),
            preferred_element_type=jnp.float32,
        )
        out[0, f] = got[0:LANES]
        out[1, f] = got[LANES : 2 * LANES]


def correlate_own(block, where_all, own, fine, columns, norm):
    listed, width = block.shape

    def kernel(spot, *refs):
        own_kernel(fine, norm, *refs)

    return pl.pallas_call(
        kernel,
        grid_spec=pltpu.PrefetchScalarGridSpec(
            num_scalar_prefetch=1,
            grid=(1,),
            in_specs=[
                pl.BlockSpec((1, 1, listed), lambda i, s: (s[0], 0, 0)),
                pl.BlockSpec((listed, width), lambda i, s: (0, 0)),
            ],
            out_specs=[
                pl.BlockSpec((2 * LANES, width), lambda i, s: (0, 0)),
                pl.BlockSpec((2, fine, LANES, LANES), lambda i, s: (0, 0, 0, 0)),
            ],
        ),
        out_shape=[
            jax.ShapeDtypeStruct((2 * LANES, width), jnp.bfloat16),
            jax.ShapeDtypeStruct((2, fine, LANES, columns), jnp.float32),
        ],
        compiler_params=pltpu.CompilerParams(vmem_limit_bytes=24 * 1024 * 1024),
        cost_estimate=pl.CostEstimate(flops=10**9, bytes_accessed=4 * 10**6, transcendentals=0),
        name="own_block",
    )(own.reshape(1), where_all, block)


def correlate_pair(result, sides, block, where_all, other, offset, fine):
    listed, width = block.shape
    spots = jnp.stack([other, offset]).astype(jnp.int32)

    def kernel(*refs):
        pair_kernel(fine, *refs)

    return pl.pallas_call(
        kernel,
        grid_spec=pltpu.PrefetchScalarGridSpec(
            num_scalar_prefetch=1,
            grid=(1,),
            in_specs=[
                pl.BlockSpec((1, 1, listed), lambda i, s: (s[0], 0, 0)),
                pl.BlockSpec((2 * LANES, width), lambda i, s: (0, 0)),
                pl.BlockSpec((listed, width), lambda i, s: (0, 0)),
                pl.BlockSpec(memory_space=pl.ANY),
            ],
            out_specs=pl.BlockSpec((2, fine, LANES, LANES), lambda i, s: (0, 0, 0, s[1])),
        ),
        out_shape=jax.ShapeDtypeStruct(result.shape, result.dtype),
        input_output_aliases={4: 0},
        compiler_params=pltpu.CompilerParams(vmem_limit_bytes=24 * 1024 * 1024),
        cost_estimate=pl.CostEstimate(flops=10**9, bytes_accessed=4 * 10**6, transcendentals=0),
        name="pair_block",
    )(spots, where_all, sides, block, result)


def moved(value, axis, steps):
    count = lax.axis_size(axis)
    return lax.ppermute(value, axis, [(s, (s + steps) % count) for s in range(count)])


def shards(voltages, filter_taps, sample_counts, keep_list):
    spectra_len = voltages.shape[3] // FFT - TAPS + 1
    chan_count = lax.axis_size("chan")
    x_count, z_count, y_count = (lax.axis_size(a) for a in ("x", "zh", "y"))
    blocks = x_count * z_count * y_count
    half_count = blocks // 2 + 1
    in_count = voltages.shape[0]
    group, x, z, y = (lax.axis_index(a) for a in ("chan", "x", "zh", "y"))
    cap = keep_list.shape[2]

    every_list = lax.all_gather(keep_list, ("x", "zh", "y", "chan"), axis=0, tiled=True)
    my_lists = lax.dynamic_index_in_dim(every_list, group, 1, keepdims=False)
    my_lists = my_lists.reshape(blocks, chan_count, cap)
    first_row = in_count * jnp.arange(chan_count, dtype=jnp.int32)[:, None]
    where_all = jnp.where(my_lists < in_count, my_lists + first_row, 1 << 20)
    where_all = where_all.reshape(blocks, 1, chan_count * cap)

    outgoing = channelize(voltages, filter_taps, sample_counts, keep_list[0], spectra_len)
    incoming = lax.all_to_all(outgoing, "chan", split_axis=0, concat_axis=0, tiled=True)
    own = incoming.reshape(chan_count * cap, outgoing.shape[2])
    fine = 8

    def number(dx, zz, yy):
        return ((x + dx) % x_count * z_count + zz) * y_count + yy

    me = number(0, z, y)
    sides, result = correlate_own(
        own, where_all, me, fine, half_count * LANES, 1.0 / math.sqrt(spectra_len)
    )

    def pair(result, block, other):
        return correlate_pair(result, sides, block, where_all, other, (other - me) % blocks, fine)

    up, down, far = (y + 1) % y_count, (y + 3) % y_count, (y + 2) % y_count
    flip = 1 - z
    odd = y % 2 == 1
    swap_a = [(0, 1), (1, 0), (2, 3), (3, 2)]
    swap_b = [(0, 3), (3, 0), (1, 2), (2, 1)]

    def relay_a(from_up, from_down):
        return lax.ppermute(jnp.where(odd, from_up, from_down), "y", swap_a)

    def relay_b(from_up, from_down):
        return lax.ppermute(jnp.where(odd, from_down, from_up), "y", swap_b)

    one = moved(own, "x", -1)
    two = moved(one, "x", -1)
    one_up = moved(one, "y", -1)
    one_down = moved(one, "y", 1)
    one_z = moved(one, "zh", 1)
    cross = moved(jnp.where(z == 1, own, two), "zh", 1)
    near_up = moved(jnp.where(y == 0, two, own), "y", -1)
    near_down = moved(jnp.where(y == y_count - 1, own, two), "y", 1)
    cross_up = moved(cross, "y", -1)
    cross_down = moved(cross, "y", 1)
    onez_up = moved(one_up, "zh", 1)
    one_far = relay_b(one_up, one_down)
    near_far = relay_a(near_up, near_down)
    onez_down = moved(one_down, "zh", 1)
    cross_far = relay_b(cross_up, cross_down)
    onez_far = relay_a(onez_up, onez_down)

    def near(yy):
        return number(jnp.where(yy > y, 0, 2), z, yy)

    def crossed(yy):
        return number(jnp.where(z == 0, 0, 2), flip, yy)

    for block, other in (
        (one, number(1, z, y)),
        (two, number(2, z, y)),
        (one_up, number(1, z, up)),
        (one_down, number(1, z, down)),
        (one_z, number(1, flip, y)),
        (near_up, near(up)),
        (near_down, near(down)),
        (cross, crossed(y)),
        (cross_up, crossed(up)),
        (cross_down, crossed(down)),
        (onez_up, number(1, flip, up)),
        (one_far, number(1, z, far)),
        (near_far, near(far)),
        (onez_down, number(1, flip, down)),
        (cross_far, crossed(far)),
        (onez_far, number(1, flip, far)),
    ):
        result = pair(result, block, other)
    return result


def solution(mesh):
    fine_mesh = Mesh(mesh.devices.reshape(4, 4, 2, 4), ("chan", "x", "zh", "y"))
    blk = ("x", "zh", "y")
    in_specs = (
        P(blk + ("chan",), None, None, None),
        P(),
        P(blk + ("chan",), None),
        P(blk + ("chan",), None, None),
    )
    out_specs = P(None, "chan", blk, None)
    return jax.shard_map(
        shards, mesh=fine_mesh, in_specs=in_specs, out_specs=out_specs, check_vma=False
    )
```

```python
import math

import jax
import jax.numpy as jnp
import numpy as np
from jax import lax
from jax.experimental import pallas as pl
from jax.experimental.pallas import tpu as pltpu
from jax.sharding import Mesh
from jax.sharding import PartitionSpec as P

TAPS = 16
FFT = 16
STEP = 8
LANES = 128
CHUNKS = LANES // STEP
UNUSED = 512


def trig_table():
    table = np.zeros((2, 2, LANES, 8, 2, STEP), np.float64)
    point = np.arange(LANES) % FFT
    for half in range(2):
        for fine in range(8):
            angle = 2.0 * math.pi * ((8 * half + fine) * point % FFT) / FFT
            cosine, sine = np.cos(angle)[:, None], np.sin(angle)[:, None]
            table[half, 0, :, fine, 0] = cosine
            table[half, 0, :, fine, 1] = -sine
            table[half, 1, :, fine, 0] = sine
            table[half, 1, :, fine, 1] = cosine
    return table.reshape(2, 2 * LANES, LANES).astype(np.float32)


def channelize_kernel(spectra_len, cap, volt, lists, counts, taps, trig, out, square, frames, weights):
    samples = volt.shape[1]
    in_count = counts.shape[1]
    tiles = -(-samples // LANES)
    listed = 2 * cap
    point_row = lax.broadcasted_iota(jnp.int32, (LANES, LANES), 0) // FFT
    spec_lane = lax.broadcasted_iota(jnp.int32, (LANES, LANES), 1) % STEP
    lag = point_row - spec_lane
    by_row = jnp.concatenate([taps[...]] * (LANES // FFT), axis=1).T
    column = [jnp.broadcast_to(by_row[:, m : m + 1], (LANES, LANES)) for m in range(TAPS)]
    for part in range(3):
        shaped = jnp.zeros((LANES, LANES), jnp.float32)
        for m in range(TAPS):
            shaped = jnp.where(lag == m - STEP * part, column[m], shaped)
        both = jnp.concatenate([shaped, shaped], axis=0)
        for half in range(2):
            exact = both * trig[half]
            high = exact.astype(jnp.bfloat16)
            low = (exact - high.astype(jnp.float32)).astype(jnp.bfloat16)
            weights[half, part, :, 0:LANES] = high
            weights[half, part, :, LANES : 2 * LANES] = low
    square[...] = jnp.zeros(square.shape, square.dtype)
    square[0:4, 0:cap] = lists[0].astype(jnp.float32)
    by_slot = square[...].T
    entry = [by_slot[0:cap, g : g + 1].astype(jnp.int32) for g in range(4)]
    gains = jnp.sqrt(samples / (FFT * counts[...].astype(jnp.float32)))
    inputs = lax.broadcasted_iota(jnp.int32, (cap, in_count), 1)
    lanes = lax.broadcasted_iota(jnp.int32, (cap, LANES), 1)
    picks = []
    for half in range(2):
        for part in range(2):
            for coarse in range(2):
                row = entry[2 * coarse + half] * 4 + (2 * coarse + part)
                picks.append((row == lanes).astype(jnp.float32))
    pick = jnp.concatenate(picks, axis=0).astype(jnp.bfloat16)
    for tile in range(tiles):
        width = min(LANES, samples - tile * LANES)
        piece = volt[:, tile * LANES : tile * LANES + width]
        if width < LANES:
            piece = jnp.concatenate([piece, jnp.zeros((LANES, LANES - width), piece.dtype)], axis=1)
        got = jnp.dot(pick, piece, preferred_element_type=jnp.float32).astype(jnp.bfloat16)
        for half in range(2):
            base = 2 * half * listed
            here = slice(tile * listed, (tile + 1) * listed)
            frames[half, here, 0:LANES] = got[base : base + listed]
            frames[half, here, LANES : 2 * LANES] = got[base + listed : base + 2 * listed]
    chunk = lax.broadcasted_iota(jnp.int32, (listed, LANES), 1) // STEP
    for half in range(2):
        factors = []
        for coarse in range(2):
            spot = entry[2 * coarse + half]
            chosen = jnp.where(spot == inputs, gains[coarse : coarse + 1, :], 0.0)
            factors.append(jnp.sum(chosen, axis=1, keepdims=True))
            told = jnp.where(spot < in_count, spot, UNUSED).astype(jnp.float32)
            told = jnp.broadcast_to(told, (cap, LANES)).astype(jnp.bfloat16)
            out[2 * coarse + half, :, 16 * spectra_len : 16 * spectra_len + LANES] = told
        gain = jnp.concatenate(factors, axis=0)
        for quarter in range(spectra_len // LANES):
            total = None
            for part in range(3):
                first = (quarter * CHUNKS + part) * listed
                term = jnp.dot(
                    frames[half, first : first + CHUNKS * listed, :],
                    weights[half, part],
                    preferred_element_type=jnp.float32,
                )
                total = term if total is None else total + term
            summed = total[:, 0:LANES] + total[:, LANES : 2 * LANES]
            lines = [summed[n * listed : (n + 1) * listed] * gain for n in range(CHUNKS)]
            bit = 1
            while bit < CHUNKS:
                keep = (chunk & bit) == 0
                fresh = list(lines)
                for n in range(CHUNKS):
                    if n & bit == 0:
                        one, two = lines[n], lines[n | bit]
                        fresh[n] = jnp.where(keep, one, pltpu.roll(two, bit * STEP, 1))
                        fresh[n | bit] = jnp.where(keep, pltpu.roll(one, LANES - bit * STEP, 1), two)
                lines = fresh
                bit *= 2
            for n in range(CHUNKS):
                lane = n * spectra_len + quarter * LANES
                value = lines[n].astype(jnp.bfloat16)
                out[half, :, lane : lane + LANES] = value[0:cap]
                out[half + 2, :, lane : lane + LANES] = value[cap : 2 * cap]


def channelize(voltages, filter_taps, sample_counts, keep_list, spectra_len):
    in_count, coarse, _, samples = voltages.shape
    groups, cap = keep_list.shape[1:]
    volt = voltages.reshape(in_count * coarse * 2, samples)
    row_width = 8 * 2 * spectra_len + LANES
    tiles = -(-samples // LANES)

    def kernel(*refs):
        channelize_kernel(spectra_len, cap, *refs)

    return pl.pallas_call(
        kernel,
        out_shape=jax.ShapeDtypeStruct((groups, cap, row_width), jnp.bfloat16),
        scratch_shapes=[
            pltpu.VMEM((LANES, LANES), jnp.float32),
            pltpu.VMEM((2, tiles * 2 * cap, 2 * LANES), jnp.bfloat16),
            pltpu.VMEM((2, 3, 2 * LANES, 2 * LANES), jnp.bfloat16),
        ],
        compiler_params=pltpu.CompilerParams(vmem_limit_bytes=32 * 1024 * 1024),
        cost_estimate=pl.CostEstimate(flops=4 * 10**9, bytes_accessed=3 * 10**6, transcendentals=0),
        name="channelize",
    )(volt, keep_list, sample_counts.T, filter_taps, trig_table())


def row_places(block, in_count, cap, width):
    listed = block.shape[0]
    told = block[:, width : width + 1].astype(jnp.float32).astype(jnp.int32)
    place = told + lax.broadcasted_iota(jnp.int32, (listed, 1), 0) // cap * in_count
    one_hot = lax.broadcasted_iota(jnp.int32, (listed, LANES), 1) == place
    return one_hot.astype(jnp.float32).T.astype(jnp.bfloat16)


def with_turned(value):
    half = value.shape[1] // 2
    turned = jnp.concatenate([value[:, half:], -value[:, :half]], axis=1)
    return jnp.concatenate([value, turned], axis=0)


def group_kernel(fine, cap, in_count, norm, picked, first, *refs):
    refs = list(refs)
    spots = refs.pop(0)
    side = None if first else refs.pop(0)
    arrays = [[refs.pop(0) for _ in range(2 if two else 1)] for two in picked]
    if not first:
        refs.pop(0)
    out = refs.pop(0)
    if first:
        side_out = refs.pop(0)
    else:
        token = refs.pop(0)
    buf, sems = refs
    count = len(picked)
    width = (arrays[0][0].shape[1] - LANES) // fine
    both_numbers = (((1,), (1,)), ((), ()))

    def rows(n, lanes):
        if picked[n]:
            return jnp.where(spots[count + n] == 1, arrays[n][0][:, lanes], arrays[n][1][:, lanes])
        return arrays[n][0][:, lanes]

    copies = []
    every = [row_places(rows(n, slice(fine * width, fine * width + LANES)), in_count, cap, 0) for n in range(count)]
    for f in range(fine):
        lanes = slice(f * width, (f + 1) * width)
        full = [
            jnp.dot(every[n], rows(n, lanes), preferred_element_type=jnp.float32).astype(jnp.bfloat16)
            for n in range(count)
        ]
        if first:
            own = (full[0].astype(jnp.float32) * norm).astype(jnp.bfloat16)
            side_out[:, lanes] = own
        else:
            own = side[:, lanes]
        stacked = jnp.concatenate(full, axis=0) if count > 1 else full[0]
        got = lax.dot_general(with_turned(own), stacked, both_numbers, preferred_element_type=jnp.float32)
        for n in range(count):
            buf[n, 0, f] = got[0:LANES, n * LANES : (n + 1) * LANES]
            buf[n, 1, f] = got[LANES : 2 * LANES, n * LANES : (n + 1) * LANES]
            column = pl.ds(pl.multiple_of(spots[n] * LANES, LANES), LANES)
            copy = pltpu.make_async_copy(buf.at[n, :, f], out.at[:, f, :, column], sems.at[n, f])
            copy.start()
            copies.append(copy)
    if not first:
        token[...] = jnp.zeros(token.shape, token.dtype)
    for copy in copies:
        copy.wait()


def correlate(result, side, blocks, offsets, sizes):
    fine, cap, in_count, columns, norm = sizes
    first = side is None
    picked = [isinstance(block, tuple) for block in blocks]
    flags = [block[0].astype(jnp.int32) if two else jnp.int32(0) for block, two in zip(blocks, picked)]
    arrays = [a for block, two in zip(blocks, picked) for a in (block[1:] if two else (block,))]
    spots = jnp.stack([jnp.int32(o) for o in offsets] + flags)
    count = len(blocks)
    width = arrays[0].shape[1] - LANES
    vmem = pl.BlockSpec(memory_space=pltpu.VMEM)
    anywhere = pl.BlockSpec(memory_space=pl.ANY)

    def kernel(*refs):
        group_kernel(fine, cap, in_count, norm, picked, first, *refs)

    whole = jax.ShapeDtypeStruct((2, fine, LANES, columns), jnp.float32)
    extra = jax.ShapeDtypeStruct((LANES, width), jnp.bfloat16) if first else jax.ShapeDtypeStruct((8, LANES), jnp.float32)
    operands = [spots] + ([] if first else [side]) + arrays + ([] if first else [result])
    return pl.pallas_call(
        kernel,
        in_specs=[pl.BlockSpec(memory_space=pltpu.SMEM)]
        + [vmem] * (len(arrays) + (0 if first else 1))
        + ([] if first else [anywhere]),
        out_specs=[anywhere, vmem],
        out_shape=[whole, extra],
        scratch_shapes=[
            pltpu.VMEM((count, 2, fine, LANES, LANES), jnp.float32),
            pltpu.SemaphoreType.DMA((count, fine)),
        ],
        input_output_aliases={} if first else {len(operands) - 1: 0},
        compiler_params=pltpu.CompilerParams(vmem_limit_bytes=24 * 1024 * 1024),
        cost_estimate=pl.CostEstimate(flops=10**8 * count, bytes_accessed=10**5 * count, transcendentals=0),
        name="own_block" if first else "pair_blocks",
    )(*operands)


def moved(value, axis, steps):
    count = lax.axis_size(axis)
    return lax.ppermute(value, axis, [(s, (s + steps) % count) for s in range(count)])


def down_x(value, rows):
    xs, ys = lax.axis_size("x"), lax.axis_size("y")
    pairs = [(x * ys + y, (x - 1) % xs * ys + y) for x in range(xs) for y in rows]
    return lax.ppermute(value, ("x", "y"), pairs)


def after(value, token):
    return lax.optimization_barrier((value, token))[0]


def shards(voltages, filter_taps, sample_counts, keep_list):
    spectra_len = voltages.shape[3] // FFT - TAPS + 1
    x_count, z_count, y_count = (lax.axis_size(a) for a in ("x", "zh", "y"))
    blocks = x_count * z_count * y_count
    x, z, y = (lax.axis_index(a) for a in ("x", "zh", "y"))
    cap = keep_list.shape[2]

    outgoing = channelize(voltages, filter_taps, sample_counts, keep_list, spectra_len)
    incoming = lax.all_to_all(outgoing, "chan", split_axis=0, concat_axis=0, tiled=True)
    own = incoming.reshape(-1, outgoing.shape[2])
    columns = (blocks // 2 + 1) * LANES
    sizes = (8, cap, voltages.shape[0], columns, 1.0 / math.sqrt(spectra_len))

    def offset(dx, zz, yy):
        other = ((x + dx) % x_count * z_count + zz) * y_count + yy
        return (other - (x * z_count + z) * y_count - y) % blocks

    up, down, far = (y + 1) % y_count, (y + 3) % y_count, (y + 2) % y_count
    flip = 1 - z

    def near(yy):
        return offset(jnp.where(yy > y, 0, 2), z, yy)

    def crossed(yy):
        return offset(jnp.where(z == 0, 0, 2), flip, yy)

    one = moved(own, "x", -1)
    own_up = moved(own, "y", -1)
    own_down = moved(own, "y", 1)
    result, side = correlate(None, None, [own], [jnp.int32(0)], sizes)
    one_up = moved(one, "y", -1)
    one_down = moved(one, "y", 1)
    two = moved(one, "x", -1)
    one_z = moved(one, "zh", 1)
    result, token = correlate(result, side, [one], [offset(1, z, y)], sizes)
    cross = moved(after(jnp.where(z == 1, own, two), token), "zh", 1)
    one_far = moved(after(one_up, token), "y", -1)
    onez_down = moved(after(one_z, token), "y", 1)
    two_down = down_x(after(one_down, token), (1, 2, 3))
    result, token = correlate(
        result,
        side,
        [two, one_up, one_down, one_z],
        [offset(2, z, y), offset(1, z, up), offset(1, z, down), offset(1, flip, y)],
        sizes,
    )
    cross_up = moved(after(cross, token), "y", -1)
    cross_down = moved(after(cross, token), "y", 1)
    onez_up = moved(after(one_up, token), "zh", 1)
    two_up = down_x(after(one_up, token), (3,))
    two_far = down_x(after(one_far, token), (2, 3))
    result, token = correlate(
        result,
        side,
        [one_far, onez_down, cross, (y == 0, own_down, two_down)],
        [offset(1, z, far), offset(1, flip, down), crossed(y), near(down)],
        sizes,
    )
    cross_far = moved(after(cross_up, token), "y", -1)
    own_far = lax.ppermute(after(own_down, token), "y", [(3, 0), (0, 1)])
    onez_far = moved(after(one_far, token), "zh", 1)
    result, token = correlate(
        result,
        side,
        [cross_up, cross_down, onez_up, (y == y_count - 1, two_up, own_up)],
        [crossed(up), crossed(down), offset(1, flip, up), near(up)],
        sizes,
    )
    result, token = correlate(
        result,
        side,
        [cross_far, onez_far, (y < 2, own_far, two_far)],
        [crossed(far), offset(1, flip, far), near(far)],
        sizes,
    )
    return result


def solution(mesh):
    fine_mesh = Mesh(mesh.devices.reshape(4, 4, 2, 4), ("chan", "x", "zh", "y"))
    blk = ("x", "zh", "y")
    in_specs = (
        P(blk + ("chan",), None, None, None),
        P(),
        P(blk + ("chan",), None),
        P(blk + ("chan",), None, None),
    )
    out_specs = P(None, "chan", blk, None)
    return jax.shard_map(
        shards, mesh=fine_mesh, in_specs=in_specs, out_specs=out_specs, check_vma=False
    )
```

```python
import math

import jax
import jax.numpy as jnp
import numpy as np
from jax import lax
from jax.experimental import pallas as pl
from jax.experimental.pallas import tpu as pltpu
from jax.sharding import Mesh
from jax.sharding import PartitionSpec as P

TAPS = 16
FFT = 16
STEP = 8
LANES = 128
CHUNKS = LANES // STEP
UNUSED = 512


def trig_table():
    table = np.zeros((2, 2, LANES, 8, 2, STEP), np.float64)
    point = np.arange(LANES) % FFT
    for half in range(2):
        for fine in range(8):
            angle = 2.0 * math.pi * ((8 * half + fine) * point % FFT) / FFT
            cosine, sine = np.cos(angle)[:, None], np.sin(angle)[:, None]
            table[half, 0, :, fine, 0] = cosine
            table[half, 0, :, fine, 1] = -sine
            table[half, 1, :, fine, 0] = sine
            table[half, 1, :, fine, 1] = cosine
    return table.reshape(2, 2 * LANES, LANES).astype(np.float32)


def channelize_kernel(spectra_len, cap, volt, lists_far, counts_far, taps_far, trig_far, out, *scratch):
    lists, counts, taps, trig, sems, square, frames, weights = scratch
    fars, nears = (lists_far, counts_far, taps_far, trig_far), (lists, counts, taps, trig)
    copies = [pltpu.make_async_copy(f, n, sems.at[i]) for i, (f, n) in enumerate(zip(fars, nears))]
    for copy in copies:
        copy.start()
    for copy in copies:
        copy.wait()
    samples = volt.shape[1]
    in_count = counts.shape[1]
    tiles = -(-samples // LANES)
    listed = 2 * cap
    point_row = lax.broadcasted_iota(jnp.int32, (LANES, LANES), 0) // FFT
    spec_lane = lax.broadcasted_iota(jnp.int32, (LANES, LANES), 1) % STEP
    lag = point_row - spec_lane
    by_row = jnp.concatenate([taps[...]] * (LANES // FFT), axis=1).T
    column = [jnp.broadcast_to(by_row[:, m : m + 1], (LANES, LANES)) for m in range(TAPS)]
    for part in range(3):
        shaped = jnp.zeros((LANES, LANES), jnp.float32)
        for m in range(TAPS):
            shaped = jnp.where(lag == m - STEP * part, column[m], shaped)
        both = jnp.concatenate([shaped, shaped], axis=0)
        for half in range(2):
            exact = both * trig[half]
            high = exact.astype(jnp.bfloat16)
            low = (exact - high.astype(jnp.float32)).astype(jnp.bfloat16)
            weights[half, part, :, 0:LANES] = high
            weights[half, part, :, LANES : 2 * LANES] = low
    square[...] = jnp.zeros(square.shape, square.dtype)
    square[0:4, 0:cap] = lists[0].astype(jnp.float32)
    by_slot = square[...].T
    entry = [by_slot[0:cap, g : g + 1].astype(jnp.int32) for g in range(4)]
    gains = jnp.sqrt(samples / (FFT * counts[...].astype(jnp.float32)))
    inputs = lax.broadcasted_iota(jnp.int32, (cap, in_count), 1)
    lanes = lax.broadcasted_iota(jnp.int32, (cap, LANES), 1)
    picks = []
    for half in range(2):
        for part in range(2):
            for coarse in range(2):
                row = entry[2 * coarse + half] * 4 + (2 * coarse + part)
                picks.append((row == lanes).astype(jnp.float32))
    pick = jnp.concatenate(picks, axis=0).astype(jnp.bfloat16)
    for tile in range(tiles):
        width = min(LANES, samples - tile * LANES)
        piece = volt[:, tile * LANES : tile * LANES + width]
        if width < LANES:
            piece = jnp.concatenate([piece, jnp.zeros((LANES, LANES - width), piece.dtype)], axis=1)
        got = jnp.dot(pick, piece, preferred_element_type=jnp.float32).astype(jnp.bfloat16)
        for half in range(2):
            base = 2 * half * listed
            here = slice(tile * listed, (tile + 1) * listed)
            frames[half, here, 0:LANES] = got[base : base + listed]
            frames[half, here, LANES : 2 * LANES] = got[base + listed : base + 2 * listed]
    chunk = lax.broadcasted_iota(jnp.int32, (listed, LANES), 1) // STEP
    for half in range(2):
        factors = []
        for coarse in range(2):
            spot = entry[2 * coarse + half]
            chosen = jnp.where(spot == inputs, gains[coarse : coarse + 1, :], 0.0)
            factors.append(jnp.sum(chosen, axis=1, keepdims=True))
            told = jnp.where(spot < in_count, spot, UNUSED).astype(jnp.float32)
            told = jnp.broadcast_to(told, (cap, LANES)).astype(jnp.bfloat16)
            out[2 * coarse + half, :, 16 * spectra_len : 16 * spectra_len + LANES] = told
        gain = jnp.concatenate(factors, axis=0)
        for quarter in range(spectra_len // LANES):
            total = None
            for part in range(3):
                first = (quarter * CHUNKS + part) * listed
                term = jnp.dot(
                    frames[half, first : first + CHUNKS * listed, :],
                    weights[half, part],
                    preferred_element_type=jnp.float32,
                )
                total = term if total is None else total + term
            summed = total[:, 0:LANES] + total[:, LANES : 2 * LANES]
            lines = [summed[n * listed : (n + 1) * listed] * gain for n in range(CHUNKS)]
            bit = 1
            while bit < CHUNKS:
                keep = (chunk & bit) == 0
                fresh = list(lines)
                for n in range(CHUNKS):
                    if n & bit == 0:
                        one, two = lines[n], lines[n | bit]
                        fresh[n] = jnp.where(keep, one, pltpu.roll(two, bit * STEP, 1))
                        fresh[n | bit] = jnp.where(keep, pltpu.roll(one, LANES - bit * STEP, 1), two)
                lines = fresh
                bit *= 2
            for n in range(CHUNKS):
                lane = n * spectra_len + quarter * LANES
                value = lines[n].astype(jnp.bfloat16)
                out[half, :, lane : lane + LANES] = value[0:cap]
                out[half + 2, :, lane : lane + LANES] = value[cap : 2 * cap]


def channelize(voltages, filter_taps, sample_counts, keep_list, spectra_len):
    in_count, coarse, _, samples = voltages.shape
    groups, cap = keep_list.shape[1:]
    volt = voltages.reshape(in_count * coarse * 2, samples)
    row_width = 8 * 2 * spectra_len + LANES
    tiles = -(-samples // LANES)

    def kernel(*refs):
        channelize_kernel(spectra_len, cap, *refs)

    return pl.pallas_call(
        kernel,
        out_shape=jax.ShapeDtypeStruct((groups, cap, row_width), jnp.bfloat16),
        in_specs=[pl.BlockSpec(memory_space=pltpu.VMEM)] + [pl.BlockSpec(memory_space=pl.ANY)] * 4,
        scratch_shapes=[
            pltpu.VMEM(keep_list.shape, jnp.int32),
            pltpu.VMEM((coarse, in_count), jnp.int32),
            pltpu.VMEM(filter_taps.shape, jnp.float32),
            pltpu.VMEM((2, 2 * LANES, LANES), jnp.float32),
            pltpu.SemaphoreType.DMA((4,)),
            pltpu.VMEM((LANES, LANES), jnp.float32),
            pltpu.VMEM((2, tiles * 2 * cap, 2 * LANES), jnp.bfloat16),
            pltpu.VMEM((2, 3, 2 * LANES, 2 * LANES), jnp.bfloat16),
        ],
        compiler_params=pltpu.CompilerParams(vmem_limit_bytes=32 * 1024 * 1024),
        cost_estimate=pl.CostEstimate(flops=4 * 10**9, bytes_accessed=3 * 10**6, transcendentals=0),
        name="channelize",
    )(volt, keep_list, sample_counts.T, filter_taps, trig_table())


def row_places(block, in_count, cap, width):
    listed = block.shape[0]
    told = block[:, width : width + 1].astype(jnp.float32).astype(jnp.int32)
    place = told + lax.broadcasted_iota(jnp.int32, (listed, 1), 0) // cap * in_count
    one_hot = lax.broadcasted_iota(jnp.int32, (listed, LANES), 1) == place
    return one_hot.astype(jnp.float32).T.astype(jnp.bfloat16)


def with_turned(value):
    half = value.shape[1] // 2
    turned = jnp.concatenate([value[:, half:], -value[:, :half]], axis=1)
    return jnp.concatenate([value, turned], axis=0)


def group_kernel(fine, cap, in_count, norm, picked, first, *refs):
    refs = list(refs)
    spots = refs.pop(0)
    side = None if first else refs.pop(0)
    arrays = [[refs.pop(0) for _ in range(2 if two else 1)] for two in picked]
    if not first:
        refs.pop(0)
    out = refs.pop(0)
    if first:
        side_out = refs.pop(0)
    else:
        token = refs.pop(0)
    full, buf, sems = refs
    count = len(picked)
    width = (arrays[0][0].shape[1] - LANES) // fine
    both_numbers = (((1,), (1,)), ((), ()))

    def rows(n, lanes):
        if picked[n]:
            return jnp.where(spots[count + n] == 1, arrays[n][0][:, lanes], arrays[n][1][:, lanes])
        return arrays[n][0][:, lanes]

    copies = []
    for n in range(count):
        told = rows(n, slice(fine * width, fine * width + LANES))
        spread = row_places(told, in_count, cap, 0)
        placed = jnp.dot(spread, rows(n, slice(0, fine * width)), preferred_element_type=jnp.float32)
        full[n * LANES : (n + 1) * LANES] = placed.astype(jnp.bfloat16)
    for f in range(fine):
        lanes = slice(f * width, (f + 1) * width)
        if first:
            own = (full[0:LANES, lanes].astype(jnp.float32) * norm).astype(jnp.bfloat16)
            side_out[:, lanes] = own
        else:
            own = side[:, lanes]
        got = lax.dot_general(with_turned(own), full[:, lanes], both_numbers, preferred_element_type=jnp.float32)
        for n in range(count):
            buf[n, 0, f] = got[0:LANES, n * LANES : (n + 1) * LANES]
            buf[n, 1, f] = got[LANES : 2 * LANES, n * LANES : (n + 1) * LANES]
            column = pl.ds(pl.multiple_of(spots[n] * LANES, LANES), LANES)
            copy = pltpu.make_async_copy(buf.at[n, :, f], out.at[:, f, :, column], sems.at[n, f])
            copy.start()
            copies.append(copy)
    if not first:
        token[...] = jnp.zeros(token.shape, token.dtype)
    for copy in copies:
        copy.wait()


def correlate(result, side, blocks, offsets, sizes):
    fine, cap, in_count, columns, norm = sizes
    first = side is None
    picked = [isinstance(block, tuple) for block in blocks]
    flags = [block[0].astype(jnp.int32) if two else jnp.int32(0) for block, two in zip(blocks, picked)]
    arrays = [a for block, two in zip(blocks, picked) for a in (block[1:] if two else (block,))]
    spots = jnp.stack([jnp.int32(o) for o in offsets] + flags)
    count = len(blocks)
    width = arrays[0].shape[1] - LANES
    vmem = pl.BlockSpec(memory_space=pltpu.VMEM)
    anywhere = pl.BlockSpec(memory_space=pl.ANY)

    def kernel(*refs):
        group_kernel(fine, cap, in_count, norm, picked, first, *refs)

    whole = jax.ShapeDtypeStruct((2, fine, LANES, columns), jnp.float32)
    extra = jax.ShapeDtypeStruct((LANES, width), jnp.bfloat16) if first else jax.ShapeDtypeStruct((8, LANES), jnp.float32)
    operands = [spots] + ([] if first else [side]) + arrays + ([] if first else [result])
    return pl.pallas_call(
        kernel,
        in_specs=[pl.BlockSpec(memory_space=pltpu.SMEM)]
        + [vmem] * (len(arrays) + (0 if first else 1))
        + ([] if first else [anywhere]),
        out_specs=[anywhere, vmem],
        out_shape=[whole, extra],
        scratch_shapes=[
            pltpu.VMEM((count * LANES, width), jnp.bfloat16),
            pltpu.VMEM((count, 2, fine, LANES, LANES), jnp.float32),
            pltpu.SemaphoreType.DMA((count, fine)),
        ],
        input_output_aliases={} if first else {len(operands) - 1: 0},
        compiler_params=pltpu.CompilerParams(vmem_limit_bytes=24 * 1024 * 1024),
        cost_estimate=pl.CostEstimate(flops=10**8 * count, bytes_accessed=10**5 * count, transcendentals=0),
        name="own_block" if first else "pair_blocks",
    )(*operands)


def moved(value, axis, steps):
    count = lax.axis_size(axis)
    return lax.ppermute(value, axis, [(s, (s + steps) % count) for s in range(count)])


def down_x(value, rows):
    xs, ys = lax.axis_size("x"), lax.axis_size("y")
    pairs = [(x * ys + y, (x - 1) % xs * ys + y) for x in range(xs) for y in rows]
    return lax.ppermute(value, ("x", "y"), pairs)


def after(value, *tokens):
    return lax.optimization_barrier((value,) + tokens)[0]


def shards(voltages, filter_taps, sample_counts, keep_list):
    spectra_len = voltages.shape[3] // FFT - TAPS + 1
    x_count, z_count, y_count = (lax.axis_size(a) for a in ("x", "zh", "y"))
    blocks = x_count * z_count * y_count
    x, z, y = (lax.axis_index(a) for a in ("x", "zh", "y"))
    cap = keep_list.shape[2]

    outgoing = channelize(voltages, filter_taps, sample_counts, keep_list, spectra_len)
    incoming = lax.all_to_all(outgoing, "chan", split_axis=0, concat_axis=0, tiled=True)
    own = incoming.reshape(-1, outgoing.shape[2])
    columns = (blocks // 2 + 1) * LANES
    sizes = (8, cap, voltages.shape[0], columns, 1.0 / math.sqrt(spectra_len))

    def offset(dx, zz, yy):
        other = ((x + dx) % x_count * z_count + zz) * y_count + yy
        return (other - (x * z_count + z) * y_count - y) % blocks

    up, down, far = (y + 1) % y_count, (y + 3) % y_count, (y + 2) % y_count
    flip = 1 - z

    def near(yy):
        return offset(jnp.where(yy > y, 0, 2), z, yy)

    def crossed(yy):
        return offset(jnp.where(z == 0, 0, 2), flip, yy)

    one = moved(own, "x", -1)
    own_z = moved(own, "zh", 1)
    own_up = lax.ppermute(own, "y", [(1, 0), (2, 1), (3, 2)])
    own_down = lax.ppermute(own, "y", [(2, 3), (3, 0)])
    result, side = correlate(None, None, [own], [jnp.int32(0)], sizes)
    later = after(one, side)
    one_up = moved(later, "y", -1)
    one_down = moved(later, "y", 1)
    beyond = moved(after(own_z, side), "x", -2)
    one_z = moved(later, "zh", 1)
    result, token = correlate(result, side, [after(one, own_up, own_down)], [offset(1, z, y)], sizes)
    cross = jnp.where(z == 0, own_z, beyond)
    one_far = moved(after(one_up, token), "y", -1)
    cross_down = moved(after(cross, token), "y", 1)
    onez_down = moved(after(one_down, token), "zh", 1)
    two_down = down_x(after(one_down, token), (1, 2, 3))
    result, token = correlate(
        result,
        side,
        [one_up, one_down, one_z, cross],
        [offset(1, z, up), offset(1, z, down), offset(1, flip, y), crossed(y)],
        sizes,
    )
    cross_up = moved(after(cross, token), "y", -1)
    cross_far = moved(after(cross_down, token), "y", 1)
    onez_far = moved(after(one_far, token), "zh", 1)
    two_far = down_x(after(one_far, token), (2, 3))
    result, token = correlate(
        result,
        side,
        [(y == 0, own_down, two_down), cross_down, one_far, onez_down],
        [near(down), crossed(down), offset(1, z, far), offset(1, flip, down)],
        sizes,
    )
    onez_up = moved(after(one_z, token), "y", -1)
    own_far = lax.ppermute(after(own_down, token), "y", [(3, 0), (0, 1)])
    two = moved(after(beyond, token), "zh", 1)
    two_up = down_x(after(one_up, token), (3,))
    result, token = correlate(
        result,
        side,
        [after(cross_up, two_far), cross_far, onez_far],
        [crossed(up), crossed(far), offset(1, flip, far)],
        sizes,
    )
    result, token = correlate(
        result,
        side,
        [onez_up, two],
        [offset(1, flip, up), offset(2, z, y)],
        sizes,
    )
    result, token = correlate(
        result,
        side,
        [(y == y_count - 1, two_up, own_up), (y < 2, own_far, two_far)],
        [near(up), near(far)],
        sizes,
    )
    return result


def solution(mesh):
    fine_mesh = Mesh(mesh.devices.reshape(4, 4, 2, 4), ("chan", "x", "zh", "y"))
    blk = ("x", "zh", "y")
    in_specs = (
        P(blk + ("chan",), None, None, None),
        P(),
        P(blk + ("chan",), None),
        P(blk + ("chan",), None, None),
    )
    out_specs = P(None, "chan", blk, None)
    return jax.shard_map(
        shards, mesh=fine_mesh, in_specs=in_specs, out_specs=out_specs, check_vma=False
    )
```

```python
import math

import jax
import jax.numpy as jnp
import numpy as np
from jax import lax
from jax.experimental import pallas as pl
from jax.experimental.pallas import tpu as pltpu
from jax.sharding import Mesh
from jax.sharding import PartitionSpec as P

TAPS = 16
FFT = 16
STEP = 8
LANES = 128
CHUNKS = LANES // STEP
UNUSED = 512


def trig_table():
    table = np.zeros((2, 2, LANES, 8, 2, STEP), np.float64)
    point = np.arange(LANES) % FFT
    for half in range(2):
        for fine in range(8):
            angle = 2.0 * math.pi * ((8 * half + fine) * point % FFT) / FFT
            cosine, sine = np.cos(angle)[:, None], np.sin(angle)[:, None]
            table[half, 0, :, fine, 0] = cosine
            table[half, 0, :, fine, 1] = -sine
            table[half, 1, :, fine, 0] = sine
            table[half, 1, :, fine, 1] = cosine
    return table.reshape(2, 2 * LANES, LANES).astype(np.float32)


def channelize_kernel(spectra_len, cap, volt, lists_far, counts_far, taps_far, trig_far, out, *scratch):
    lists, counts, taps, trig, sems, square, frames, weights = scratch
    fars, nears = (lists_far, counts_far, taps_far, trig_far), (lists, counts, taps, trig)
    copies = [pltpu.make_async_copy(f, n, sems.at[i]) for i, (f, n) in enumerate(zip(fars, nears))]
    for copy in copies:
        copy.start()
    for copy in copies:
        copy.wait()
    samples = volt.shape[1]
    in_count = counts.shape[1]
    tiles = -(-samples // LANES)
    listed = 2 * cap
    point_row = lax.broadcasted_iota(jnp.int32, (LANES, LANES), 0) // FFT
    spec_lane = lax.broadcasted_iota(jnp.int32, (LANES, LANES), 1) % STEP
    lag = point_row - spec_lane
    by_row = jnp.concatenate([taps[...]] * (LANES // FFT), axis=1).T
    column = [jnp.broadcast_to(by_row[:, m : m + 1], (LANES, LANES)) for m in range(TAPS)]
    for part in range(3):
        shaped = jnp.zeros((LANES, LANES), jnp.float32)
        for m in range(TAPS):
            shaped = jnp.where(lag == m - STEP * part, column[m], shaped)
        both = jnp.concatenate([shaped, shaped], axis=0)
        for half in range(2):
            exact = both * trig[half]
            high = exact.astype(jnp.bfloat16)
            low = (exact - high.astype(jnp.float32)).astype(jnp.bfloat16)
            weights[half, part, :, 0:LANES] = high
            weights[half, part, :, LANES : 2 * LANES] = low
    square[...] = jnp.zeros(square.shape, square.dtype)
    square[0:4, 0:cap] = lists[0].astype(jnp.float32)
    by_slot = square[...].T
    entry = [by_slot[0:cap, g : g + 1].astype(jnp.int32) for g in range(4)]
    gains = jnp.sqrt(samples / (FFT * counts[...].astype(jnp.float32)))
    inputs = lax.broadcasted_iota(jnp.int32, (cap, in_count), 1)
    lanes = lax.broadcasted_iota(jnp.int32, (cap, LANES), 1)
    picks = []
    for half in range(2):
        for part in range(2):
            for coarse in range(2):
                row = entry[2 * coarse + half] * 4 + (2 * coarse + part)
                picks.append((row == lanes).astype(jnp.float32))
    pick = jnp.concatenate(picks, axis=0).astype(jnp.bfloat16)
    for tile in range(tiles):
        width = min(LANES, samples - tile * LANES)
        piece = volt[:, tile * LANES : tile * LANES + width]
        if width < LANES:
            piece = jnp.concatenate([piece, jnp.zeros((LANES, LANES - width), piece.dtype)], axis=1)
        got = jnp.dot(pick, piece, preferred_element_type=jnp.float32).astype(jnp.bfloat16)
        for half in range(2):
            base = 2 * half * listed
            here = slice(tile * listed, (tile + 1) * listed)
            frames[half, here, 0:LANES] = got[base : base + listed]
            frames[half, here, LANES : 2 * LANES] = got[base + listed : base + 2 * listed]
    chunk = lax.broadcasted_iota(jnp.int32, (listed, LANES), 1) // STEP
    for half in range(2):
        factors = []
        for coarse in range(2):
            spot = entry[2 * coarse + half]
            chosen = jnp.where(spot == inputs, gains[coarse : coarse + 1, :], 0.0)
            factors.append(jnp.sum(chosen, axis=1, keepdims=True))
            told = jnp.where(spot < in_count, spot, UNUSED).astype(jnp.float32)
            told = jnp.broadcast_to(told, (cap, LANES)).astype(jnp.bfloat16)
            out[2 * coarse + half, :, 16 * spectra_len : 16 * spectra_len + LANES] = told
        gain = jnp.concatenate(factors, axis=0)
        for quarter in range(spectra_len // LANES):
            total = None
            for part in range(3):
                first = (quarter * CHUNKS + part) * listed
                term = jnp.dot(
                    frames[half, first : first + CHUNKS * listed, :],
                    weights[half, part],
                    preferred_element_type=jnp.float32,
                )
                total = term if total is None else total + term
            summed = total[:, 0:LANES] + total[:, LANES : 2 * LANES]
            lines = [summed[n * listed : (n + 1) * listed] * gain for n in range(CHUNKS)]
            bit = 1
            while bit < CHUNKS:
                keep = (chunk & bit) == 0
                fresh = list(lines)
                for n in range(CHUNKS):
                    if n & bit == 0:
                        one, two = lines[n], lines[n | bit]
                        fresh[n] = jnp.where(keep, one, pltpu.roll(two, bit * STEP, 1))
                        fresh[n | bit] = jnp.where(keep, pltpu.roll(one, LANES - bit * STEP, 1), two)
                lines = fresh
                bit *= 2
            for n in range(CHUNKS):
                lane = n * spectra_len + quarter * LANES
                value = lines[n].astype(jnp.bfloat16)
                out[half, :, lane : lane + LANES] = value[0:cap]
                out[half + 2, :, lane : lane + LANES] = value[cap : 2 * cap]


def channelize(voltages, filter_taps, sample_counts, keep_list, spectra_len):
    in_count, coarse, _, samples = voltages.shape
    groups, cap = keep_list.shape[1:]
    volt = voltages.reshape(in_count * coarse * 2, samples)
    row_width = 8 * 2 * spectra_len + LANES
    tiles = -(-samples // LANES)

    def kernel(*refs):
        channelize_kernel(spectra_len, cap, *refs)

    return pl.pallas_call(
        kernel,
        out_shape=jax.ShapeDtypeStruct((groups, cap, row_width), jnp.bfloat16),
        in_specs=[pl.BlockSpec(memory_space=pltpu.VMEM)] + [pl.BlockSpec(memory_space=pl.ANY)] * 4,
        scratch_shapes=[
            pltpu.VMEM(keep_list.shape, jnp.int32),
            pltpu.VMEM((coarse, in_count), jnp.int32),
            pltpu.VMEM(filter_taps.shape, jnp.float32),
            pltpu.VMEM((2, 2 * LANES, LANES), jnp.float32),
            pltpu.SemaphoreType.DMA((4,)),
            pltpu.VMEM((LANES, LANES), jnp.float32),
            pltpu.VMEM((2, tiles * 2 * cap, 2 * LANES), jnp.bfloat16),
            pltpu.VMEM((2, 3, 2 * LANES, 2 * LANES), jnp.bfloat16),
        ],
        compiler_params=pltpu.CompilerParams(vmem_limit_bytes=32 * 1024 * 1024),
        cost_estimate=pl.CostEstimate(flops=4 * 10**9, bytes_accessed=3 * 10**6, transcendentals=0),
        name="channelize",
    )(volt, keep_list, sample_counts.T, filter_taps, trig_table())


def row_places(block, in_count, cap, width):
    listed = block.shape[0]
    told = block[:, width : width + 1].astype(jnp.float32).astype(jnp.int32)
    place = told + lax.broadcasted_iota(jnp.int32, (listed, 1), 0) // cap * in_count
    one_hot = lax.broadcasted_iota(jnp.int32, (listed, LANES), 1) == place
    return one_hot.astype(jnp.float32).T.astype(jnp.bfloat16)


def with_turned(value):
    half = value.shape[1] // 2
    turned = jnp.concatenate([value[:, half:], -value[:, :half]], axis=1)
    return jnp.concatenate([value, turned], axis=0)


def group_kernel(fine, cap, in_count, norm, picked, first, *refs):
    refs = list(refs)
    spots = refs.pop(0)
    side = None if first else refs.pop(0)
    arrays = [[refs.pop(0) for _ in range(2 if two else 1)] for two in picked]
    if not first:
        refs.pop(0)
    out = refs.pop(0)
    if first:
        side_out = refs.pop(0)
    else:
        token = refs.pop(0)
    full, buf, sems = refs
    count = len(picked)
    width = (arrays[0][0].shape[1] - LANES) // fine
    both_numbers = (((1,), (1,)), ((), ()))

    def rows(n, lanes):
        if picked[n]:
            return jnp.where(spots[count + n] == 1, arrays[n][0][:, lanes], arrays[n][1][:, lanes])
        return arrays[n][0][:, lanes]

    copies, part = [], fine // 2
    for n in range(count):
        told = rows(n, slice(fine * width, fine * width + LANES))
        spread = row_places(told, in_count, cap, 0)
        placed = jnp.dot(spread, rows(n, slice(0, fine * width)), preferred_element_type=jnp.float32)
        full[n * LANES : (n + 1) * LANES] = placed.astype(jnp.bfloat16)
    for f in range(fine):
        lanes = slice(f * width, (f + 1) * width)
        if first:
            own = (full[0:LANES, lanes].astype(jnp.float32) * norm).astype(jnp.bfloat16)
            side_out[:, lanes] = own
        else:
            own = side[:, lanes]
        got = lax.dot_general(with_turned(own), full[:, lanes], both_numbers, preferred_element_type=jnp.float32)
        for n in range(count):
            buf[n, 0, f] = got[0:LANES, n * LANES : (n + 1) * LANES]
            buf[n, 1, f] = got[LANES : 2 * LANES, n * LANES : (n + 1) * LANES]
            if f % part == part - 1:
                now = pl.ds(f - part + 1, part)
                column = pl.ds(pl.multiple_of(spots[n] * LANES, LANES), LANES)
                copy = pltpu.make_async_copy(buf.at[n, :, now], out.at[:, now, :, column], sems.at[n, f // part])
                copy.start()
                copies.append(copy)
    if not first:
        token[...] = jnp.zeros(token.shape, token.dtype)
    for copy in copies:
        copy.wait()


def correlate(result, side, blocks, offsets, sizes):
    fine, cap, in_count, columns, norm = sizes
    first = side is None
    picked = [isinstance(block, tuple) for block in blocks]
    flags = [block[0].astype(jnp.int32) if two else jnp.int32(0) for block, two in zip(blocks, picked)]
    arrays = [a for block, two in zip(blocks, picked) for a in (block[1:] if two else (block,))]
    spots = jnp.stack([jnp.int32(o) for o in offsets] + flags)
    count = len(blocks)
    width = arrays[0].shape[1] - LANES
    vmem = pl.BlockSpec(memory_space=pltpu.VMEM)
    anywhere = pl.BlockSpec(memory_space=pl.ANY)

    def kernel(*refs):
        group_kernel(fine, cap, in_count, norm, picked, first, *refs)

    whole = jax.ShapeDtypeStruct((2, fine, LANES, columns), jnp.float32)
    extra = jax.ShapeDtypeStruct((LANES, width), jnp.bfloat16) if first else jax.ShapeDtypeStruct((8, LANES), jnp.float32)
    operands = [spots] + ([] if first else [side]) + arrays + ([] if first else [result])
    return pl.pallas_call(
        kernel,
        in_specs=[pl.BlockSpec(memory_space=pltpu.SMEM)]
        + [vmem] * (len(arrays) + (0 if first else 1))
        + ([] if first else [anywhere]),
        out_specs=[anywhere, vmem],
        out_shape=[whole, extra],
        scratch_shapes=[
            pltpu.VMEM((count * LANES, width), jnp.bfloat16),
            pltpu.VMEM((count, 2, fine, LANES, LANES), jnp.float32),
            pltpu.SemaphoreType.DMA((count, 2)),
        ],
        input_output_aliases={} if first else {len(operands) - 1: 0},
        compiler_params=pltpu.CompilerParams(vmem_limit_bytes=24 * 1024 * 1024),
        cost_estimate=pl.CostEstimate(flops=10**8 * count, bytes_accessed=10**5 * count, transcendentals=0),
        name="own_block" if first else "pair_blocks",
    )(*operands)


def moved(value, axis, steps):
    count = lax.axis_size(axis)
    return lax.ppermute(value, axis, [(s, (s + steps) % count) for s in range(count)])


def down_x(value, rows):
    xs, ys = lax.axis_size("x"), lax.axis_size("y")
    pairs = [(x * ys + y, (x - 1) % xs * ys + y) for x in range(xs) for y in rows]
    return lax.ppermute(value, ("x", "y"), pairs)


def after(value, *tokens):
    return lax.optimization_barrier((value,) + tokens)[0]


def shards(voltages, filter_taps, sample_counts, keep_list):
    spectra_len = voltages.shape[3] // FFT - TAPS + 1
    x_count, z_count, y_count = (lax.axis_size(a) for a in ("x", "zh", "y"))
    blocks = x_count * z_count * y_count
    x, z, y = (lax.axis_index(a) for a in ("x", "zh", "y"))
    cap = keep_list.shape[2]

    outgoing = channelize(voltages, filter_taps, sample_counts, keep_list, spectra_len)
    incoming = lax.all_to_all(outgoing, "chan", split_axis=0, concat_axis=0, tiled=True)
    own = incoming.reshape(-1, outgoing.shape[2])
    columns = (blocks // 2 + 1) * LANES
    sizes = (8, cap, voltages.shape[0], columns, 1.0 / math.sqrt(spectra_len))

    def offset(dx, zz, yy):
        other = ((x + dx) % x_count * z_count + zz) * y_count + yy
        return (other - (x * z_count + z) * y_count - y) % blocks

    up, down, far = (y + 1) % y_count, (y + 3) % y_count, (y + 2) % y_count
    flip = 1 - z

    def near(yy):
        return offset(jnp.where(yy > y, 0, 2), z, yy)

    def crossed(yy):
        return offset(jnp.where(z == 0, 0, 2), flip, yy)

    one = moved(own, "x", -1)
    own_z = moved(own, "zh", 1)
    own_up = lax.ppermute(own, "y", [(1, 0), (2, 1), (3, 2)])
    own_down = lax.ppermute(own, "y", [(2, 3), (3, 0)])
    result, side = correlate(None, None, [own], [jnp.int32(0)], sizes)
    later = after(one, side)
    one_up = moved(later, "y", -1)
    one_down = moved(later, "y", 1)
    beyond = moved(after(own_z, side), "x", -2)
    one_z = moved(later, "zh", 1)
    result, token = correlate(result, side, [after(one, own_up, own_down)], [offset(1, z, y)], sizes)
    cross = jnp.where(z == 0, own_z, beyond)
    one_far = moved(after(one_up, token), "y", -1)
    cross_down = moved(after(cross, token), "y", 1)
    onez_down = moved(after(one_down, token), "zh", 1)
    two_down = down_x(after(one_down, token), (1, 2, 3))
    result, token = correlate(
        result,
        side,
        [one_up, one_down, one_z, cross],
        [offset(1, z, up), offset(1, z, down), offset(1, flip, y), crossed(y)],
        sizes,
    )
    cross_up = moved(after(cross, token), "y", -1)
    cross_far = moved(after(cross_down, token), "y", 1)
    onez_far = moved(after(one_far, token), "zh", 1)
    two_far = down_x(after(one_far, token), (2, 3))
    result, token = correlate(
        result,
        side,
        [(y == 0, own_down, two_down), cross_down, one_far, onez_down],
        [near(down), crossed(down), offset(1, z, far), offset(1, flip, down)],
        sizes,
    )
    onez_up = moved(after(one_z, token), "y", -1)
    own_far = lax.ppermute(after(own_down, token), "y", [(3, 0), (0, 1)])
    two = moved(after(beyond, token), "zh", 1)
    two_up = down_x(after(one_up, token), (3,))
    result, token = correlate(
        result,
        side,
        [after(cross_up, two_far), cross_far, onez_far],
        [crossed(up), crossed(far), offset(1, flip, far)],
        sizes,
    )
    result, token = correlate(
        result,
        side,
        [onez_up, two],
        [offset(1, flip, up), offset(2, z, y)],
        sizes,
    )
    result, token = correlate(
        result,
        side,
        [(y == y_count - 1, two_up, own_up), (y < 2, own_far, two_far)],
        [near(up), near(far)],
        sizes,
    )
    return result


def solution(mesh):
    fine_mesh = Mesh(mesh.devices.reshape(4, 4, 2, 4), ("chan", "x", "zh", "y"))
    blk = ("x", "zh", "y")
    in_specs = (
        P(blk + ("chan",), None, None, None),
        P(),
        P(blk + ("chan",), None),
        P(blk + ("chan",), None, None),
    )
    out_specs = P(None, "chan", blk, None)
    return jax.shard_map(
        shards, mesh=fine_mesh, in_specs=in_specs, out_specs=out_specs, check_vma=False
    )
```

```python
import math

import jax
import jax.numpy as jnp
from jax import lax
from jax.experimental import pallas as pl
from jax.experimental.pallas import tpu as pltpu
from jax.sharding import Mesh
from jax.sharding import PartitionSpec as P

TAPS = 16
FFT = 16
STEP = 8
LANES = 128
CHUNKS = LANES // STEP
UNUSED = 512


def trig_factors(half):
    shape = (2 * LANES, LANES)
    row = lax.broadcasted_iota(jnp.int32, shape, 0)
    lane = lax.broadcasted_iota(jnp.int32, shape, 1)
    part_in, part_out = row // LANES, lane // STEP % 2
    turn = (8 * half + lane // (2 * STEP)) * (row % FFT) + 4 * (part_out - part_in) + FFT
    turn = turn % FFT
    turn = jnp.minimum(turn, FFT - turn)
    value = jnp.full(shape, 1.0, jnp.float32)
    for step in range(1, FFT // 2 + 1):
        cosine = 0.0 if 4 * step == FFT else math.cos(2.0 * math.pi * step / FFT)
        value = jnp.where(turn == step, jnp.float32(cosine), value)
    return value


def channelize_kernel(spectra_len, cap, volt, small, out, square, frames, weights):
    groups, coarse, in_count = 4, 2, volt.shape[0] // 4
    lists = small[0:groups, 0:cap]
    counts = small[groups : groups + coarse, 0:in_count]
    taps = small[groups + coarse : groups + coarse + TAPS, 0:FFT]
    trig = [trig_factors(half) for half in range(2)]
    samples = volt.shape[1]
    tiles = -(-samples // LANES)
    listed = 2 * cap
    point_row = lax.broadcasted_iota(jnp.int32, (LANES, LANES), 0) // FFT
    spec_lane = lax.broadcasted_iota(jnp.int32, (LANES, LANES), 1) % STEP
    lag = point_row - spec_lane
    by_row = jnp.concatenate([taps] * (LANES // FFT), axis=1).T
    column = [jnp.broadcast_to(by_row[:, m : m + 1], (LANES, LANES)) for m in range(TAPS)]
    for part in range(3):
        shaped = jnp.zeros((LANES, LANES), jnp.float32)
        for m in range(TAPS):
            shaped = jnp.where(lag == m - STEP * part, column[m], shaped)
        both = jnp.concatenate([shaped, shaped], axis=0)
        for half in range(2):
            exact = both * trig[half]
            high = exact.astype(jnp.bfloat16)
            low = (exact - high.astype(jnp.float32)).astype(jnp.bfloat16)
            weights[half, part, :, 0:LANES] = high
            weights[half, part, :, LANES : 2 * LANES] = low
    square[...] = jnp.zeros(square.shape, square.dtype)
    square[0:4, 0:cap] = lists
    by_slot = square[...].T
    entry = [by_slot[0:cap, g : g + 1].astype(jnp.int32) for g in range(4)]
    gains = jnp.sqrt(samples / (FFT * counts))
    inputs = lax.broadcasted_iota(jnp.int32, (cap, in_count), 1)
    lanes = lax.broadcasted_iota(jnp.int32, (cap, LANES), 1)
    picks = []
    for half in range(2):
        for part in range(2):
            for coarse in range(2):
                row = entry[2 * coarse + half] * 4 + (2 * coarse + part)
                picks.append((row == lanes).astype(jnp.float32))
    pick = jnp.concatenate(picks, axis=0).astype(jnp.bfloat16)
    for tile in range(tiles):
        width = min(LANES, samples - tile * LANES)
        piece = volt[:, tile * LANES : tile * LANES + width]
        if width < LANES:
            piece = jnp.concatenate([piece, jnp.zeros((LANES, LANES - width), piece.dtype)], axis=1)
        got = jnp.dot(pick, piece, preferred_element_type=jnp.float32).astype(jnp.bfloat16)
        for half in range(2):
            base = 2 * half * listed
            here = slice(tile * listed, (tile + 1) * listed)
            frames[half, here, 0:LANES] = got[base : base + listed]
            frames[half, here, LANES : 2 * LANES] = got[base + listed : base + 2 * listed]
    chunk = lax.broadcasted_iota(jnp.int32, (listed, LANES), 1) // STEP
    for half in range(2):
        factors = []
        for coarse in range(2):
            spot = entry[2 * coarse + half]
            chosen = jnp.where(spot == inputs, gains[coarse : coarse + 1, :], 0.0)
            factors.append(jnp.sum(chosen, axis=1, keepdims=True))
            told = jnp.where(spot < in_count, spot, UNUSED).astype(jnp.float32)
            told = jnp.broadcast_to(told, (cap, LANES)).astype(jnp.bfloat16)
            out[2 * coarse + half, :, 16 * spectra_len : 16 * spectra_len + LANES] = told
        gain = jnp.concatenate(factors, axis=0)
        for quarter in range(spectra_len // LANES):
            total = None
            for part in range(3):
                first = (quarter * CHUNKS + part) * listed
                term = jnp.dot(
                    frames[half, first : first + CHUNKS * listed, :],
                    weights[half, part],
                    preferred_element_type=jnp.float32,
                )
                total = term if total is None else total + term
            summed = total[:, 0:LANES] + total[:, LANES : 2 * LANES]
            lines = [summed[n * listed : (n + 1) * listed] * gain for n in range(CHUNKS)]
            bit = 1
            while bit < CHUNKS:
                keep = (chunk & bit) == 0
                fresh = list(lines)
                for n in range(CHUNKS):
                    if n & bit == 0:
                        one, two = lines[n], lines[n | bit]
                        fresh[n] = jnp.where(keep, one, pltpu.roll(two, bit * STEP, 1))
                        fresh[n | bit] = jnp.where(keep, pltpu.roll(one, LANES - bit * STEP, 1), two)
                lines = fresh
                bit *= 2
            for n in range(CHUNKS):
                lane = n * spectra_len + quarter * LANES
                value = lines[n].astype(jnp.bfloat16)
                out[half, :, lane : lane + LANES] = value[0:cap]
                out[half + 2, :, lane : lane + LANES] = value[cap : 2 * cap]


def channelize(voltages, filter_taps, sample_counts, keep_list, spectra_len):
    in_count, coarse, _, samples = voltages.shape
    groups, cap = keep_list.shape[1:]
    volt = voltages.reshape(in_count * coarse * 2, samples)
    parts = (keep_list[0].astype(jnp.float32), sample_counts.T.astype(jnp.float32), filter_taps)
    small = jnp.concatenate([jnp.pad(p, ((0, 0), (0, LANES - p.shape[1]))) for p in parts], axis=0)
    row_width = 8 * 2 * spectra_len + LANES
    tiles = -(-samples // LANES)

    def kernel(*refs):
        channelize_kernel(spectra_len, cap, *refs)

    return pl.pallas_call(
        kernel,
        out_shape=jax.ShapeDtypeStruct((groups, cap, row_width), jnp.bfloat16),
        scratch_shapes=[
            pltpu.VMEM((LANES, LANES), jnp.float32),
            pltpu.VMEM((2, tiles * 2 * cap, 2 * LANES), jnp.bfloat16),
            pltpu.VMEM((2, 3, 2 * LANES, 2 * LANES), jnp.bfloat16),
        ],
        compiler_params=pltpu.CompilerParams(vmem_limit_bytes=32 * 1024 * 1024),
        cost_estimate=pl.CostEstimate(flops=4 * 10**9, bytes_accessed=3 * 10**6, transcendentals=0),
        name="channelize",
    )(volt, small)


def row_places(block, in_count, cap, width):
    listed = block.shape[0]
    told = block[:, width : width + 1].astype(jnp.float32).astype(jnp.int32)
    place = told + lax.broadcasted_iota(jnp.int32, (listed, 1), 0) // cap * in_count
    one_hot = lax.broadcasted_iota(jnp.int32, (listed, LANES), 1) == place
    return one_hot.astype(jnp.float32).T.astype(jnp.bfloat16)


def with_turned(value):
    half = value.shape[1] // 2
    turned = jnp.concatenate([value[:, half:], -value[:, :half]], axis=1)
    return jnp.concatenate([value, turned], axis=0)


def group_kernel(fine, cap, in_count, norm, picked, first, *refs):
    refs = list(refs)
    spots = refs.pop(0)
    side = None if first else refs.pop(0)
    arrays = [[refs.pop(0) for _ in range(2 if two else 1)] for two in picked]
    if not first:
        refs.pop(0)
    out = refs.pop(0)
    if first:
        side_out = refs.pop(0)
    else:
        token = refs.pop(0)
    full, buf, sems = refs
    count = len(picked)
    width = (arrays[0][0].shape[1] - LANES) // fine
    both_numbers = (((1,), (1,)), ((), ()))

    def rows(n, lanes):
        if picked[n]:
            return jnp.where(spots[count + n] == 1, arrays[n][0][:, lanes], arrays[n][1][:, lanes])
        return arrays[n][0][:, lanes]

    copies, part = [], fine // 2
    for n in range(count):
        told = rows(n, slice(fine * width, fine * width + LANES))
        spread = row_places(told, in_count, cap, 0)
        placed = jnp.dot(spread, rows(n, slice(0, fine * width)), preferred_element_type=jnp.float32)
        full[n * LANES : (n + 1) * LANES] = placed.astype(jnp.bfloat16)
    for f in range(fine):
        lanes = slice(f * width, (f + 1) * width)
        if first:
            own = (full[0:LANES, lanes].astype(jnp.float32) * norm).astype(jnp.bfloat16)
            side_out[:, lanes] = own
        else:
            own = side[:, lanes]
        got = lax.dot_general(with_turned(own), full[:, lanes], both_numbers, preferred_element_type=jnp.float32)
        for n in range(count):
            buf[n, 0, f] = got[0:LANES, n * LANES : (n + 1) * LANES]
            buf[n, 1, f] = got[LANES : 2 * LANES, n * LANES : (n + 1) * LANES]
            if f % part == part - 1:
                now = pl.ds(f - part + 1, part)
                column = pl.ds(pl.multiple_of(spots[n] * LANES, LANES), LANES)
                copy = pltpu.make_async_copy(buf.at[n, :, now], out.at[:, now, :, column], sems.at[n, f // part])
                copy.start()
                copies.append(copy)
    if not first:
        token[...] = jnp.zeros(token.shape, token.dtype)
    for copy in copies:
        copy.wait()


def correlate(result, side, blocks, offsets, sizes):
    fine, cap, in_count, columns, norm = sizes
    first = side is None
    picked = [isinstance(block, tuple) for block in blocks]
    flags = [block[0].astype(jnp.int32) if two else jnp.int32(0) for block, two in zip(blocks, picked)]
    arrays = [a for block, two in zip(blocks, picked) for a in (block[1:] if two else (block,))]
    spots = jnp.stack([jnp.int32(o) for o in offsets] + flags)
    count = len(blocks)
    width = arrays[0].shape[1] - LANES
    vmem = pl.BlockSpec(memory_space=pltpu.VMEM)
    anywhere = pl.BlockSpec(memory_space=pl.ANY)

    def kernel(*refs):
        group_kernel(fine, cap, in_count, norm, picked, first, *refs)

    whole = jax.ShapeDtypeStruct((2, fine, LANES, columns), jnp.float32)
    extra = jax.ShapeDtypeStruct((LANES, width), jnp.bfloat16) if first else jax.ShapeDtypeStruct((8, LANES), jnp.float32)
    operands = [spots] + ([] if first else [side]) + arrays + ([] if first else [result])
    return pl.pallas_call(
        kernel,
        in_specs=[pl.BlockSpec(memory_space=pltpu.SMEM)]
        + [vmem] * (len(arrays) + (0 if first else 1))
        + ([] if first else [anywhere]),
        out_specs=[anywhere, vmem],
        out_shape=[whole, extra],
        scratch_shapes=[
            pltpu.VMEM((count * LANES, width), jnp.bfloat16),
            pltpu.VMEM((count, 2, fine, LANES, LANES), jnp.float32),
            pltpu.SemaphoreType.DMA((count, 2)),
        ],
        input_output_aliases={} if first else {len(operands) - 1: 0},
        compiler_params=pltpu.CompilerParams(vmem_limit_bytes=24 * 1024 * 1024),
        cost_estimate=pl.CostEstimate(flops=10**8 * count, bytes_accessed=10**5 * count, transcendentals=0),
        name="own_block" if first else "pair_blocks",
    )(*operands)


def moved(value, axis, steps):
    count = lax.axis_size(axis)
    return lax.ppermute(value, axis, [(s, (s + steps) % count) for s in range(count)])


def down_x(value, rows):
    xs, ys = lax.axis_size("x"), lax.axis_size("y")
    pairs = [(x * ys + y, (x - 1) % xs * ys + y) for x in range(xs) for y in rows]
    return lax.ppermute(value, ("x", "y"), pairs)


def after(value, *tokens):
    return lax.optimization_barrier((value,) + tokens)[0]


def shards(voltages, filter_taps, sample_counts, keep_list):
    spectra_len = voltages.shape[3] // FFT - TAPS + 1
    x_count, z_count, y_count = (lax.axis_size(a) for a in ("x", "zh", "y"))
    blocks = x_count * z_count * y_count
    x, z, y = (lax.axis_index(a) for a in ("x", "zh", "y"))
    cap = keep_list.shape[2]

    outgoing = channelize(voltages, filter_taps, sample_counts, keep_list, spectra_len)
    incoming = lax.all_to_all(outgoing, "chan", split_axis=0, concat_axis=0, tiled=True)
    own = incoming.reshape(-1, outgoing.shape[2])
    columns = (blocks // 2 + 1) * LANES
    sizes = (8, cap, voltages.shape[0], columns, 1.0 / math.sqrt(spectra_len))

    def offset(dx, zz, yy):
        other = ((x + dx) % x_count * z_count + zz) * y_count + yy
        return (other - (x * z_count + z) * y_count - y) % blocks

    up, down, far = (y + 1) % y_count, (y + 3) % y_count, (y + 2) % y_count
    flip = 1 - z

    def near(yy):
        return offset(jnp.where(yy > y, 0, 2), z, yy)

    def crossed(yy):
        return offset(jnp.where(z == 0, 0, 2), flip, yy)

    one = moved(own, "x", -1)
    own_z = moved(own, "zh", 1)
    own_up = lax.ppermute(own, "y", [(1, 0), (2, 1), (3, 2)])
    own_down = lax.ppermute(own, "y", [(2, 3), (3, 0)])
    result, side = correlate(None, None, [own], [jnp.int32(0)], sizes)
    later = after(one, side)
    one_up = moved(later, "y", -1)
    one_down = moved(later, "y", 1)
    beyond = moved(after(own_z, side), "x", -2)
    one_z = moved(later, "zh", 1)
    result, token = correlate(result, side, [after(one, own_up, own_down)], [offset(1, z, y)], sizes)
    cross = jnp.where(z == 0, own_z, beyond)
    one_far = moved(after(one_up, token), "y", -1)
    cross_down = moved(after(cross, token), "y", 1)
    onez_down = moved(after(one_down, token), "zh", 1)
    two_down = down_x(after(one_down, token), (1, 2, 3))
    result, token = correlate(
        result,
        side,
        [one_up, one_down, one_z, cross],
        [offset(1, z, up), offset(1, z, down), offset(1, flip, y), crossed(y)],
        sizes,
    )
    cross_up = moved(after(cross, token), "y", -1)
    cross_far = moved(after(cross_down, token), "y", 1)
    onez_far = moved(after(one_far, token), "zh", 1)
    two_far = down_x(after(one_far, token), (2, 3))
    result, token = correlate(
        result,
        side,
        [(y == 0, own_down, two_down), cross_down, one_far, onez_down],
        [near(down), crossed(down), offset(1, z, far), offset(1, flip, down)],
        sizes,
    )
    onez_up = moved(after(one_z, token), "y", -1)
    own_far = lax.ppermute(after(own_down, token), "y", [(3, 0), (0, 1)])
    two = moved(after(beyond, token), "zh", 1)
    two_up = down_x(after(one_up, token), (3,))
    result, token = correlate(
        result,
        side,
        [after(cross_up, two_far), cross_far, onez_far],
        [crossed(up), crossed(far), offset(1, flip, far)],
        sizes,
    )
    result, token = correlate(
        result,
        side,
        [onez_up, two],
        [offset(1, flip, up), offset(2, z, y)],
        sizes,
    )
    result, token = correlate(
        result,
        side,
        [(y == y_count - 1, two_up, own_up), (y < 2, own_far, two_far)],
        [near(up), near(far)],
        sizes,
    )
    return result


def solution(mesh):
    fine_mesh = Mesh(mesh.devices.reshape(4, 4, 2, 4), ("chan", "x", "zh", "y"))
    blk = ("x", "zh", "y")
    in_specs = (
        P(blk + ("chan",), None, None, None),
        P(),
        P(blk + ("chan",), None),
        P(blk + ("chan",), None, None),
    )
    out_specs = P(None, "chan", blk, None)
    return jax.shard_map(
        shards, mesh=fine_mesh, in_specs=in_specs, out_specs=out_specs, check_vma=False
    )
```

```python
import math

import jax
import jax.numpy as jnp
from jax import lax
from jax.experimental import pallas as pl
from jax.experimental.pallas import tpu as pltpu
from jax.sharding import Mesh
from jax.sharding import PartitionSpec as P

TAPS = 16
FFT = 16
STEP = 8
LANES = 128
CHUNKS = LANES // STEP
UNUSED = 512


def trig_factors(half):
    shape = (2 * LANES, LANES)
    row = lax.broadcasted_iota(jnp.int32, shape, 0)
    lane = lax.broadcasted_iota(jnp.int32, shape, 1)
    part_in, part_out = row // LANES, lane // STEP % 2
    turn = (8 * half + lane // (2 * STEP)) * (row % FFT) + 4 * (part_out - part_in) + FFT
    turn = turn % FFT
    turn = jnp.minimum(turn, FFT - turn)
    value = jnp.full(shape, 1.0, jnp.float32)
    for step in range(1, FFT // 2 + 1):
        cosine = 0.0 if 4 * step == FFT else math.cos(2.0 * math.pi * step / FFT)
        value = jnp.where(turn == step, jnp.float32(cosine), value)
    return value


def channelize_kernel(spectra_len, cap, volt, small, out, square, frames, weights):
    groups, coarse, in_count = 4, 2, volt.shape[0] // 4
    lists = small[0:groups, 0:cap]
    counts = small[groups : groups + coarse, 0:in_count]
    taps = small[groups + coarse : groups + coarse + TAPS, 0:FFT]
    trig = [trig_factors(half) for half in range(2)]
    samples = volt.shape[1]
    tiles = -(-samples // LANES)
    listed = 2 * cap
    point_row = lax.broadcasted_iota(jnp.int32, (LANES, LANES), 0) // FFT
    spec_lane = lax.broadcasted_iota(jnp.int32, (LANES, LANES), 1) % STEP
    lag = point_row - spec_lane
    by_row = jnp.concatenate([taps] * (LANES // FFT), axis=1).T
    column = [jnp.broadcast_to(by_row[:, m : m + 1], (LANES, LANES)) for m in range(TAPS)]
    for part in range(3):
        shaped = jnp.zeros((LANES, LANES), jnp.float32)
        for m in range(TAPS):
            shaped = jnp.where(lag == m - STEP * part, column[m], shaped)
        both = jnp.concatenate([shaped, shaped], axis=0)
        for half in range(2):
            exact = both * trig[half]
            high = exact.astype(jnp.bfloat16)
            low = (exact - high.astype(jnp.float32)).astype(jnp.bfloat16)
            weights[half, part, :, 0:LANES] = high
            weights[half, part, :, LANES : 2 * LANES] = low
    square[...] = jnp.zeros(square.shape, square.dtype)
    square[0:4, 0:cap] = lists
    by_slot = square[...].T
    entry = [by_slot[0:cap, g : g + 1].astype(jnp.int32) for g in range(4)]
    gains = jnp.sqrt(samples / (FFT * counts))
    inputs = lax.broadcasted_iota(jnp.int32, (cap, in_count), 1)
    lanes = lax.broadcasted_iota(jnp.int32, (cap, LANES), 1)
    picks = []
    for half in range(2):
        for part in range(2):
            for coarse in range(2):
                row = entry[2 * coarse + half] * 4 + (2 * coarse + part)
                picks.append((row == lanes).astype(jnp.float32))
    pick = jnp.concatenate(picks, axis=0).astype(jnp.bfloat16)
    for tile in range(tiles):
        width = min(LANES, samples - tile * LANES)
        piece = volt[:, tile * LANES : tile * LANES + width]
        if width < LANES:
            piece = jnp.concatenate([piece, jnp.zeros((LANES, LANES - width), piece.dtype)], axis=1)
        got = jnp.dot(pick, piece, preferred_element_type=jnp.float32).astype(jnp.bfloat16)
        for half in range(2):
            base = 2 * half * listed
            here = slice(tile * listed, (tile + 1) * listed)
            frames[half, here, 0:LANES] = got[base : base + listed]
            frames[half, here, LANES : 2 * LANES] = got[base + listed : base + 2 * listed]
    chunk = lax.broadcasted_iota(jnp.int32, (listed, LANES), 1) // STEP
    for half in range(2):
        factors = []
        for coarse in range(2):
            spot = entry[2 * coarse + half]
            chosen = jnp.where(spot == inputs, gains[coarse : coarse + 1, :], 0.0)
            factors.append(jnp.sum(chosen, axis=1, keepdims=True))
            told = jnp.where(spot < in_count, spot, UNUSED).astype(jnp.float32)
            told = jnp.broadcast_to(told, (cap, LANES)).astype(jnp.bfloat16)
            out[2 * coarse + half, :, 16 * spectra_len : 16 * spectra_len + LANES] = told
        gain = jnp.concatenate(factors, axis=0)
        for quarter in range(spectra_len // LANES):
            total = None
            for part in range(3):
                first = (quarter * CHUNKS + part) * listed
                term = jnp.dot(
                    frames[half, first : first + CHUNKS * listed, :],
                    weights[half, part],
                    preferred_element_type=jnp.float32,
                )
                total = term if total is None else total + term
            summed = total[:, 0:LANES] + total[:, LANES : 2 * LANES]
            lines = [summed[n * listed : (n + 1) * listed] * gain for n in range(CHUNKS)]
            bit = 1
            while bit < CHUNKS:
                keep = (chunk & bit) == 0
                fresh = list(lines)
                for n in range(CHUNKS):
                    if n & bit == 0:
                        one, two = lines[n], lines[n | bit]
                        fresh[n] = jnp.where(keep, one, pltpu.roll(two, bit * STEP, 1))
                        fresh[n | bit] = jnp.where(keep, pltpu.roll(one, LANES - bit * STEP, 1), two)
                lines = fresh
                bit *= 2
            for n in range(CHUNKS):
                lane = n * spectra_len + quarter * LANES
                value = lines[n].astype(jnp.bfloat16)
                out[half, :, lane : lane + LANES] = value[0:cap]
                out[half + 2, :, lane : lane + LANES] = value[cap : 2 * cap]


def channelize(voltages, filter_taps, sample_counts, keep_list, spectra_len):
    in_count, coarse, _, samples = voltages.shape
    groups, cap = keep_list.shape[1:]
    volt = voltages.reshape(in_count * coarse * 2, samples)
    parts = (keep_list[0].astype(jnp.float32), sample_counts.T.astype(jnp.float32), filter_taps)
    small = jnp.concatenate([jnp.pad(p, ((0, 0), (0, LANES - p.shape[1]))) for p in parts], axis=0)
    row_width = 8 * 2 * spectra_len + LANES
    tiles = -(-samples // LANES)

    def kernel(*refs):
        channelize_kernel(spectra_len, cap, *refs)

    return pl.pallas_call(
        kernel,
        out_shape=jax.ShapeDtypeStruct((groups, cap, row_width), jnp.bfloat16),
        scratch_shapes=[
            pltpu.VMEM((LANES, LANES), jnp.float32),
            pltpu.VMEM((2, tiles * 2 * cap, 2 * LANES), jnp.bfloat16),
            pltpu.VMEM((2, 3, 2 * LANES, 2 * LANES), jnp.bfloat16),
        ],
        compiler_params=pltpu.CompilerParams(vmem_limit_bytes=32 * 1024 * 1024),
        cost_estimate=pl.CostEstimate(flops=4 * 10**9, bytes_accessed=3 * 10**6, transcendentals=0),
        name="channelize",
    )(volt, small)


def row_places(block, in_count, cap, width):
    listed = block.shape[0]
    told = block[:, width : width + 1].astype(jnp.float32).astype(jnp.int32)
    place = told + lax.broadcasted_iota(jnp.int32, (listed, 1), 0) // cap * in_count
    one_hot = lax.broadcasted_iota(jnp.int32, (listed, LANES), 1) == place
    return one_hot.astype(jnp.float32).T.astype(jnp.bfloat16)


def with_turned(value):
    half = value.shape[1] // 2
    turned = jnp.concatenate([value[:, half:], -value[:, :half]], axis=1)
    return jnp.concatenate([value, turned], axis=0)


def group_kernel(fine, cap, in_count, norm, picked, first, *refs):
    refs = list(refs)
    spots = refs.pop(0)
    side = None if first else refs.pop(0)
    arrays = [[refs.pop(0) for _ in range(2 if two else 1)] for two in picked]
    if not first:
        refs.pop(0)
    out = refs.pop(0)
    if first:
        side_out = refs.pop(0)
    else:
        token = refs.pop(0)
    full, buf, sems = refs
    count = len(picked)
    width = (arrays[0][0].shape[1] - LANES) // fine
    both_numbers = (((1,), (1,)), ((), ()))

    def rows(n, lanes):
        if picked[n]:
            return jnp.where(spots[count + n] == 1, arrays[n][0][:, lanes], arrays[n][1][:, lanes])
        return arrays[n][0][:, lanes]

    copies, part = [], fine // 2
    for n in range(count):
        told = rows(n, slice(fine * width, fine * width + LANES))
        spread = row_places(told, in_count, cap, 0)
        placed = jnp.dot(spread, rows(n, slice(0, fine * width)), preferred_element_type=jnp.float32)
        full[n * LANES : (n + 1) * LANES] = placed.astype(jnp.bfloat16)
    for f in range(fine):
        lanes = slice(f * width, (f + 1) * width)
        if first:
            own = (full[0:LANES, lanes].astype(jnp.float32) * norm).astype(jnp.bfloat16)
            side_out[:, lanes] = own
        else:
            own = side[:, lanes]
        got = lax.dot_general(with_turned(own), full[:, lanes], both_numbers, preferred_element_type=jnp.float32)
        for n in range(count):
            buf[n, 0, f] = got[0:LANES, n * LANES : (n + 1) * LANES]
            buf[n, 1, f] = got[LANES : 2 * LANES, n * LANES : (n + 1) * LANES]
            if f % part == part - 1:
                now = pl.ds(f - part + 1, part)
                column = pl.ds(pl.multiple_of(spots[n] * LANES, LANES), LANES)
                copy = pltpu.make_async_copy(buf.at[n, :, now], out.at[:, now, :, column], sems.at[n, f // part])
                copy.start()
                copies.append(copy)
    if not first:
        token[...] = jnp.zeros(token.shape, token.dtype)
    for copy in copies:
        copy.wait()


def correlate(result, side, blocks, offsets, sizes):
    fine, cap, in_count, columns, norm = sizes
    first = side is None
    picked = [isinstance(block, tuple) for block in blocks]
    flags = [block[0].astype(jnp.int32) if two else jnp.int32(0) for block, two in zip(blocks, picked)]
    arrays = [a for block, two in zip(blocks, picked) for a in (block[1:] if two else (block,))]
    spots = jnp.stack([jnp.int32(o) for o in offsets] + flags)
    count = len(blocks)
    width = arrays[0].shape[1] - LANES
    vmem = pl.BlockSpec(memory_space=pltpu.VMEM)
    anywhere = pl.BlockSpec(memory_space=pl.ANY)

    def kernel(*refs):
        group_kernel(fine, cap, in_count, norm, picked, first, *refs)

    whole = jax.ShapeDtypeStruct((2, fine, LANES, columns), jnp.float32)
    extra = jax.ShapeDtypeStruct((LANES, width), jnp.bfloat16) if first else jax.ShapeDtypeStruct((8, LANES), jnp.float32)
    operands = [spots] + ([] if first else [side]) + arrays + ([] if first else [result])
    return pl.pallas_call(
        kernel,
        in_specs=[pl.BlockSpec(memory_space=pltpu.SMEM)]
        + [vmem] * (len(arrays) + (0 if first else 1))
        + ([] if first else [anywhere]),
        out_specs=[anywhere, vmem],
        out_shape=[whole, extra],
        scratch_shapes=[
            pltpu.VMEM((count * LANES, width), jnp.bfloat16),
            pltpu.VMEM((count, 2, fine, LANES, LANES), jnp.float32),
            pltpu.SemaphoreType.DMA((count, 2)),
        ],
        input_output_aliases={} if first else {len(operands) - 1: 0},
        compiler_params=pltpu.CompilerParams(vmem_limit_bytes=24 * 1024 * 1024),
        cost_estimate=pl.CostEstimate(flops=10**8 * count, bytes_accessed=10**5 * count, transcendentals=0),
        name="own_block" if first else "pair_blocks",
    )(*operands)


def moved(value, axis, steps):
    count = lax.axis_size(axis)
    return lax.ppermute(value, axis, [(s, (s + steps) % count) for s in range(count)])


def down_x(value, rows):
    xs, ys = lax.axis_size("x"), lax.axis_size("y")
    pairs = [(x * ys + y, (x - 1) % xs * ys + y) for x in range(xs) for y in rows]
    return lax.ppermute(value, ("x", "y"), pairs)


def after(value, *tokens):
    return lax.optimization_barrier((value,) + tokens)[0]


def shards(voltages, filter_taps, sample_counts, keep_list):
    spectra_len = voltages.shape[3] // FFT - TAPS + 1
    x_count, z_count, y_count = (lax.axis_size(a) for a in ("x", "zh", "y"))
    blocks = x_count * z_count * y_count
    x, z, y = (lax.axis_index(a) for a in ("x", "zh", "y"))
    cap = keep_list.shape[2]

    outgoing = channelize(voltages, filter_taps, sample_counts, keep_list, spectra_len)
    incoming = lax.all_to_all(outgoing, "chan", split_axis=0, concat_axis=0, tiled=True)
    own = incoming.reshape(-1, outgoing.shape[2])
    columns = (blocks // 2 + 1) * LANES
    sizes = (8, cap, voltages.shape[0], columns, 1.0 / math.sqrt(spectra_len))

    def offset(dx, zz, yy):
        other = ((x + dx) % x_count * z_count + zz) * y_count + yy
        return (other - (x * z_count + z) * y_count - y) % blocks

    up, down, far = (y + 1) % y_count, (y + 3) % y_count, (y + 2) % y_count
    flip = 1 - z

    def near(yy):
        return offset(jnp.where(yy > y, 0, 2), z, yy)

    def crossed(yy):
        return offset(jnp.where(z == 0, 0, 2), flip, yy)

    one = moved(own, "x", -1)
    own_z = moved(own, "zh", 1)
    own_up = lax.ppermute(own, "y", [(1, 0), (2, 1), (3, 2)])
    own_down = lax.ppermute(own, "y", [(2, 3), (3, 0)])
    result, side = correlate(None, None, [own], [jnp.int32(0)], sizes)
    later = after(one, side)
    one_up = moved(later, "y", -1)
    one_down = moved(later, "y", 1)
    beyond = moved(after(own_z, side), "x", -2)
    one_z = moved(later, "zh", 1)
    result, token = correlate(result, side, [after(one, own_up, own_down)], [offset(1, z, y)], sizes)
    cross = jnp.where(z == 0, own_z, beyond)
    one_far = moved(after(one_up, token), "y", -1)
    cross_down = moved(after(cross, token), "y", 1)
    onez_down = moved(after(one_down, token), "zh", 1)
    two_down = down_x(after(one_down, token), (1, 2, 3))
    result, token = correlate(
        result,
        side,
        [one_up, one_down, one_z, cross],
        [offset(1, z, up), offset(1, z, down), offset(1, flip, y), crossed(y)],
        sizes,
    )
    cross_up = moved(after(cross, token), "y", -1)
    cross_far = moved(after(cross_down, token), "y", 1)
    onez_far = moved(after(one_far, token), "zh", 1)
    two_far = down_x(after(one_far, token), (2, 3))
    result, token = correlate(
        result,
        side,
        [(y == 0, own_down, two_down), cross_down, one_far, onez_down],
        [near(down), crossed(down), offset(1, z, far), offset(1, flip, down)],
        sizes,
    )
    onez_up = moved(after(one_z, token), "y", -1)
    own_far = lax.ppermute(after(own_down, token), "y", [(3, 0), (0, 1)])
    two = moved(after(beyond, token), "zh", 1)
    two_up = down_x(after(one_up, token), (3,))
    result, token = correlate(
        result,
        side,
        [after(cross_up, two_far), cross_far, onez_far],
        [crossed(up), crossed(far), offset(1, flip, far)],
        sizes,
    )
    result, token = correlate(
        result,
        side,
        [onez_up, two, (y == y_count - 1, two_up, own_up), (y < 2, own_far, two_far)],
        [offset(1, flip, up), offset(2, z, y), near(up), near(far)],
        sizes,
    )
    return result


def solution(mesh):
    fine_mesh = Mesh(mesh.devices.reshape(4, 4, 2, 4), ("chan", "x", "zh", "y"))
    blk = ("x", "zh", "y")
    in_specs = (
        P(blk + ("chan",), None, None, None),
        P(),
        P(blk + ("chan",), None),
        P(blk + ("chan",), None, None),
    )
    out_specs = P(None, "chan", blk, None)
    return jax.shard_map(
        shards, mesh=fine_mesh, in_specs=in_specs, out_specs=out_specs, check_vma=False
    )
```
